512 devices in a mesh: var: 64 (over z, x_hi, core), samp: 8 (over y, x_lo).
Axes of the slice: x: 4 (x_hi: 2, x_lo: 2; x = x_hi * 2 + x_lo), y: 4, z: 16, core: 2. Of those that a mesh axis runs over, the one named last changes fastest.
Arguments:
- observed: bfloat16 [4096, 65536], P('samp', 'var'), may hold values from -40 to 40
- pattern: int32 [512, 3], P('var'), may hold values from 0 to 511, as said below
- omega_init: bfloat16 [512, 3, 128, 128], P('var'), may hold values from -4 to 4
Outputs:
- precision: float32 [512, 3, 128, 128], P(('var', 'samp'))
The draws below stay inside these ranges and needn't reach their ends.
Inputs may be any that keep to these rules, and one draw needn't show every extreme that they name: pattern[R, 0] = R. The other two blocks of row block R belong to two different var devices among the four whose index differs from the owner of R by 1 or 2 (counted modulo the number of var devices). On every var device each of those four devices supplies the second block of exactly two of its row blocks.
All inputs are finite; a program needn't handle non-finite values.
Results may differ from the reference program's by a relative error of at most 0.0044.
Values may be sent and summed in bfloat16 or wider, within the bound.
No kernel may reach another device: no remote copies, remote signals or barrier semaphores. Data moves between devices by JAX's collectives and lax.ppermute only.
A program may use at most 64 MiB of HBM per device.

```python
import jax
import jax.numpy as jnp
from jax import lax

BLK = 128
K = 3
ITERS = 2
ROWB = 8
ROWBLOCKS = 512
VARS = 65536
SAMPLES = 4096
N_VAR = 64


def draw_observed(key, part):
    key = jax.random.fold_in(key, 11)
    keys = jax.random.split(key, 2)
    positions = jnp.arange(VARS, dtype=jnp.float32) / VARS
    trends = 1.0 + 0.35 * positions
    spread = jax.random.uniform(keys[0], (VARS,), jnp.float32)
    scales = 0.5 * jnp.exp(jnp.log(10.0) * spread) * trends
    normals = jnp.clip(jax.random.normal(keys[1], (SAMPLES, VARS), jnp.float32), -5.0, 5.0)
    values = normals * scales
    return values.astype(jnp.bfloat16)


def draw_pattern(key, part):
    key = jax.random.fold_in(key, 23)
    keys = jax.random.split(key, 3)
    orders = jax.vmap(lambda single: jax.random.permutation(single, ROWB))(jax.random.split(keys[0], N_VAR))
    leading = orders.astype(jnp.int32) % 4
    trailing = (leading + 1 + jax.random.randint(keys[1], (N_VAR, ROWB), 0, 3)) % 4
    lead_offset = leading - 2 + (leading >= 2).astype(jnp.int32)
    trail_offset = trailing - 2 + (trailing >= 2).astype(jnp.int32)
    owners = jnp.arange(N_VAR, dtype=jnp.int32)[:, None]
    within = jax.random.randint(keys[2], (N_VAR, ROWB, 2), 0, ROWB)
    first_col = (owners + lead_offset + N_VAR) % N_VAR * ROWB + within[:, :, 0]
    second_col = (owners + trail_offset + N_VAR) % N_VAR * ROWB + within[:, :, 1]
    own_col = jnp.arange(ROWBLOCKS, dtype=jnp.int32).reshape(N_VAR, ROWB)
    return jnp.stack((own_col, first_col, second_col), axis=-1).reshape(ROWBLOCKS, K).astype(jnp.int32)


def draw_omega_init(key, part):
    key = jax.random.fold_in(key, 37)
    keys = jax.random.split(key, 2)
    values = 0.5 * jnp.clip(jax.random.normal(keys[0], (ROWBLOCKS, K, BLK, BLK), jnp.float32), -5.0, 5.0)
    diagonal = 2.0 * jnp.exp(jnp.log(2.0) * jax.random.uniform(keys[1], (ROWBLOCKS, BLK), jnp.float32))
    slot_ids = jnp.arange(K)[:, None, None]
    row_ids = jnp.arange(BLK)[None, :, None]
    col_ids = jnp.arange(BLK)[None, None, :]
    diag_mask = (slot_ids == 0) & (row_ids == col_ids)
    values = jnp.where(diag_mask[None], diagonal[:, None, :, None], values)
    return values.astype(jnp.bfloat16)


def setup_inputs(seed: int = 0) -> dict:
    key_of = jax.random.split(jax.random.key(seed), 4)
    observed = draw_observed(jax.random.fold_in(key_of[3], 71), 0)
    pattern = draw_pattern(jax.random.fold_in(key_of[3], 71), 0)
    omega_init = draw_omega_init(jax.random.fold_in(key_of[3], 71), 0)
    return dict(observed=observed, pattern=pattern, omega_init=omega_init)


STEP_SCALE = 0.5
THRESHOLD = 0.25
EPSILON = 1e-06

def proximal(iterate, grad, mean_sq, diag_mask):
    step_size = STEP_SCALE / jnp.sqrt(mean_sq + EPSILON)
    stepped = iterate - step_size * grad
    shrunk = stepped - jnp.clip(stepped, -THRESHOLD, THRESHOLD)
    barrier = 0.5 * (stepped + jnp.sqrt(stepped * stepped + 4.0 * step_size))
    return jnp.where(diag_mask, barrier, shrunk)

def settle(values):
    return lax.optimization_barrier(values.astype(jnp.bfloat16)).astype(jnp.float32)

def reference(observed, pattern, omega_init):
    blocks = observed.reshape(SAMPLES, VARS // BLK, BLK)
    slot_ids = lax.broadcasted_iota(jnp.int32, (K, BLK, BLK), 0)
    row_ids = lax.broadcasted_iota(jnp.int32, (K, BLK, BLK), 1)
    col_ids = lax.broadcasted_iota(jnp.int32, (K, BLK, BLK), 2)
    diag_mask = (slot_ids == 0) & (row_ids == col_ids)
    iterate = omega_init.astype(jnp.float32)
    for iteration in range(ITERS):
        packed = settle(iterate)

        def device_rows(operands):
            omega_rows, pattern_rows = operands
            chosen = jnp.take(blocks, pattern_rows.reshape(-1).astype(jnp.int32), axis=1)
            chosen = chosen.reshape(SAMPLES, ROWB, K, BLK).astype(jnp.float32)
            weighted = settle(jnp.einsum('rkab,nrkb->rna', omega_rows, chosen))
            return jnp.einsum('rna,nrkb->rkab', weighted, chosen) / SAMPLES
        grad = lax.map(device_rows, (packed.reshape(N_VAR, ROWB, K, BLK, BLK), pattern.reshape(N_VAR, ROWB, K)))
        grad = grad.reshape(ROWBLOCKS, K, BLK, BLK)
        mean_sq = jnp.mean(grad * grad)
        iterate = proximal(iterate, grad, mean_sq, diag_mask)
    return iterate
```

```python
import jax
import jax.numpy as jnp
from jax import lax
from jax.experimental import pallas as pl
from jax.experimental.pallas import tpu as pltpu
from jax.sharding import Mesh, PartitionSpec as P

STEP_SCALE = 0.5
THRESHOLD = 0.25
EPSILON = 1e-06

AXES = ("z", "xh", "core", "y", "xl")
SIZES = (16, 2, 2, 4, 2)
VAR_AXES = ("z", "xh", "core")
SAMP_AXES = ("y", "xl")
CHUNKS = 2
ROWB = 8
K = 3
BLK = 128
SAMPLES = 4096
ENTRIES = 25165824
SAMP = 8
PAIRS = ((0, 0), (0, 1), (0, 2), (1, 1), (1, 2), (2, 2))
NPAIR = len(PAIRS)

VMEM = pl.BlockSpec(memory_space=pltpu.VMEM)
SMEM = pl.BlockSpec(memory_space=pltpu.SMEM)
ANY = pl.BlockSpec(memory_space=pl.ANY)
F32 = jnp.float32
BF16 = jnp.bfloat16


def params():
    return pltpu.CompilerParams(vmem_limit_bytes=48 * 1024 * 1024)


def gram_kernel(source, column, *refs):
    inputs = refs[: 2 + 3 * CHUNKS]
    out, held, sems = refs[2 + 3 * CHUNKS :]
    samples = held.shape[1]
    part = samples // CHUNKS
    copies = [
        pltpu.make_async_copy(inputs[0], held.at[0], sems.at[0]),
        pltpu.make_async_copy(inputs[1], held.at[1], sems.at[1]),
    ]
    for i in range(3 * CHUNKS):
        slot, chunk = 2 + i // CHUNKS, i % CHUNKS
        rows = pl.ds(chunk * part, part)
        copies.append(pltpu.make_async_copy(inputs[2 + i], held.at[slot, rows], sems.at[2 + i]))
    for copy in copies:
        copy.start()
    for copy in copies:
        copy.wait()

    def one(r, carry):
        cols = [
            held[source[r, k], :, pl.ds(pl.multiple_of(column[r, k] * BLK, BLK), BLK)]
            for k in range(K)
        ]
        for p, (i, j) in enumerate(PAIRS):
            gram = lax.dot_general(
                cols[i], cols[j], (((0,), (0,)), ((), ())), preferred_element_type=F32
            )
            out[r, p] = (gram * (1.0 / SAMPLES)).astype(BF16)
        return carry

    lax.fori_loop(0, ROWB, one, 0)


def gram(source, column, arrays):
    samples, columns = arrays[0].shape
    return pl.pallas_call(
        gram_kernel,
        out_shape=jax.ShapeDtypeStruct((ROWB, NPAIR, BLK, BLK), BF16),
        in_specs=[SMEM, SMEM] + [ANY] * len(arrays),
        out_specs=VMEM,
        scratch_shapes=[
            pltpu.VMEM((5, samples, columns), BF16),
            pltpu.SemaphoreType.DMA((len(arrays),)),
        ],
        compiler_params=params(),
        name="gram",
    )(source, column, *arrays)


def times_gram(packed, high, low):
    total = jnp.zeros((BLK, K * BLK), F32)
    for j in range(K):
        rows = slice(j * BLK, (j + 1) * BLK)
        total += jnp.dot(packed[j], high[rows, :], preferred_element_type=F32)
        total += jnp.dot(packed[j], low[rows, :], preferred_element_type=F32)
    return [total[:, k * BLK : (k + 1) * BLK] for k in range(K)]


def put_squares(grads, out):
    squares = sum(jnp.sum(g * g, axis=0, keepdims=True) for g in grads)
    out[...] = jnp.broadcast_to(squares, out.shape)


def first_kernel(parts, omega, high, low, grad, squares):
    for p, (i, j) in enumerate(PAIRS):
        block = sum(parts[s, p].astype(F32) for s in range(SAMP))
        hi = block.astype(BF16)
        lo = (block - hi.astype(F32)).astype(BF16)
        at = (pl.ds(i * BLK, BLK), pl.ds(j * BLK, BLK))
        high[at] = hi
        low[at] = lo
        if i != j:
            flipped = block.T
            hi = flipped.astype(BF16)
            lo = (flipped - hi.astype(F32)).astype(BF16)
            at = (pl.ds(j * BLK, BLK), pl.ds(i * BLK, BLK))
            high[at] = hi
            low[at] = lo
    grads = times_gram(omega, high, low)
    for k in range(K):
        grad[k] = grads[k]
    put_squares(grads, squares)


def step_of(squares):
    mean_sq = jnp.sum(squares[...]) * (1.0 / ENTRIES)
    mean_sq = jnp.full((8, BLK), mean_sq, F32)
    return (STEP_SCALE / jnp.sqrt(mean_sq + EPSILON))[0:1, :]


def proximal(iterate, grad, step, k):
    stepped = iterate - step * grad
    shrunk = stepped - jnp.clip(stepped, -THRESHOLD, THRESHOLD)
    if k:
        return shrunk
    row = lax.broadcasted_iota(jnp.int32, (BLK, BLK), 0)
    col = lax.broadcasted_iota(jnp.int32, (BLK, BLK), 1)
    barrier = 0.5 * (stepped + jnp.sqrt(stepped * stepped + 4.0 * step))
    return jnp.where(row == col, barrier, shrunk)


def second_kernel(squares, omega, grad, high, low, iterate, grad2, squares2):
    step = step_of(squares)
    packed = []
    for k in range(K):
        value = proximal(omega[k].astype(F32), grad[k], step, k)
        iterate[k] = value
        packed.append(value.astype(BF16))
    grads = times_gram(packed, high, low)
    for k in range(K):
        grad2[k] = grads[k]
    put_squares(grads, squares2)


def last_kernel(squares, iterate, grad, out):
    step = step_of(squares)
    for k in range(K):
        out[k] = proximal(iterate[k], grad[k], step, k)


def relay_kernel(rows, out):
    out[...] = jnp.broadcast_to(jnp.sum(rows[...], axis=0, keepdims=True), out.shape)


def call(kernel, shapes, *args):
    shapes = [jax.ShapeDtypeStruct(s, d) for s, d in shapes]
    return pl.pallas_call(
        kernel,
        out_shape=shapes,
        in_specs=[VMEM] * len(args),
        out_specs=[VMEM] * len(shapes),
        compiler_params=params(),
        name=kernel.__name__,
    )(*args)


def everywhere(rows):
    rows = lax.all_to_all(rows, ("xh", "y", "xl"), 0, 0, tiled=True)
    (rows,) = call(relay_kernel, [((32, BLK), F32)], rows)
    return lax.all_to_all(rows, ("z", "core"), 0, 0, tiled=True)


def swap(block, axis):
    return lax.ppermute(block, axis, [(0, 1), (1, 0)])


def along_z(block):
    depth, wide = SIZES[0], SIZES[1]
    route = []
    for z in range(depth):
        route.append((z * wide, (z + 1) % depth * wide))
        route.append((z * wide + 1, (z - 1) % depth * wide + 1))
    return lax.ppermute(block, ("z", "xh"), route)


def body(observed, pattern, omega_init):
    z, xh, core = (lax.axis_index(a) for a in VAR_AXES)
    samp = lax.axis_index("y") * 2 + lax.axis_index("xl")
    var = (z * 2 + xh) * 2 + core
    var_count = SIZES[0] * 4
    offset = (pattern // ROWB - var + var_count + 2) % var_count - 2
    near = jnp.where((offset == 1) == (core == 0), 1, 3)
    far = jnp.where((offset == 2) == (xh == 0), 2, 4)
    source = jnp.where(offset == 0, 0, jnp.where(abs(offset) == 1, near, far)).astype(jnp.int32)
    column = (pattern % ROWB).astype(jnp.int32)

    part = observed.shape[0] // CHUNKS
    partner = swap(observed, "core")
    across = [swap(observed[i * part : (i + 1) * part], "xh") for i in range(CHUNKS)]
    beyond = [along_z(a) for a in across]
    beside = [swap(jnp.where(core == xh, a, b), "core") for a, b in zip(across, beyond)]
    grams = gram(source, column, [observed, partner, *across, *beside, *beyond])
    parts = lax.all_to_all(grams, SAMP_AXES, 0, 0, tiled=True)

    omega = lax.dynamic_index_in_dim(omega_init, samp, 0, keepdims=False)
    side = K * BLK
    blocks = (K, BLK, BLK)
    high, low, grad, squares = call(
        first_kernel,
        [((side, side), BF16), ((side, side), BF16), (blocks, F32), ((16, BLK), F32)],
        parts,
        omega,
    )
    iterate, grad, squares = call(
        second_kernel,
        [(blocks, F32), (blocks, F32), ((16, BLK), F32)],
        everywhere(squares),
        omega,
        grad,
        high,
        low,
    )
    (precision,) = call(last_kernel, [(blocks, F32)], everywhere(squares), iterate, grad)
    return precision[None]


def solution(mesh):
    fine = Mesh(mesh.devices.reshape(SIZES), AXES)
    return jax.shard_map(
        body,
        mesh=fine,
        in_specs=(P(SAMP_AXES, VAR_AXES), P(VAR_AXES, None), P(VAR_AXES, None, None, None)),
        out_specs=P(AXES, None, None, None),
        check_vma=False,
    )
```

```python
import jax
import jax.numpy as jnp
from jax import lax
from jax.experimental import pallas as pl
from jax.experimental.pallas import tpu as pltpu
from jax.sharding import Mesh, PartitionSpec as P

STEP_SCALE = 0.5
THRESHOLD = 0.25
EPSILON = 1e-06

AXES = ("z", "xh", "core", "y", "xl")
SIZES = (16, 2, 2, 4, 2)
VAR_AXES = ("z", "xh", "core")
SAMP_AXES = ("y", "xl")
SIZES_OF_CHUNKS = (176, 176, 160)
CHUNKS = len(SIZES_OF_CHUNKS)
ROWB = 8
K = 3
BLK = 128
SAMPLES = 4096
ENTRIES = 25165824
SAMP = 8
CROSS = ((0, 1), (0, 2), (1, 2))
MIXED = 4 * BLK
DIAGS = 5 * BLK
GRAM_ROWS = 5 * BLK + 16

VMEM = pl.BlockSpec(memory_space=pltpu.VMEM)
SMEM = pl.BlockSpec(memory_space=pltpu.SMEM)
ANY = pl.BlockSpec(memory_space=pl.ANY)
F32 = jnp.float32
BF16 = jnp.bfloat16


def params():
    return pltpu.CompilerParams(vmem_limit_bytes=16 * 1024 * 1024)


def fetch(inputs, held, sems):
    copies = [pltpu.make_async_copy(inputs[i], held.at[i], sems.at[i]) for i in range(2)]
    for i in range(3 * CHUNKS):
        slot, chunk = 2 + i // CHUNKS, i % CHUNKS
        rows = pl.ds(sum(SIZES_OF_CHUNKS[:chunk]), SIZES_OF_CHUNKS[chunk])
        copies.append(pltpu.make_async_copy(inputs[2 + i], held.at[slot, rows], sems.at[2 + i]))
    for copy in copies:
        copy.start()
    for copy in copies:
        copy.wait()


def columns_of(held, source, column, r):
    return [
        held[source[r, k], :, pl.ds(pl.multiple_of(column[r, k] * BLK, BLK), BLK)] for k in range(K)
    ]


def dot(left, right, left_dim, right_dim):
    return lax.dot_general(
        left, right, (((left_dim,), (right_dim,)), ((), ())), preferred_element_type=F32
    )


def diagonal_mask():
    row = lax.broadcasted_iota(jnp.int32, (BLK, BLK), 0)
    col = lax.broadcasted_iota(jnp.int32, (BLK, BLK), 1)
    return row, col


def gram_kernel(source, column, *refs):
    *inputs, out, held, sems = refs
    fetch(inputs, held, sems)
    row, col = diagonal_mask()
    line = lax.broadcasted_iota(jnp.int32, (16, BLK), 0)

    def one(r, carry):
        cols = columns_of(held, source, column, r)
        scaled = [
            dot(cols[i], jnp.concatenate(cols[i:], axis=1), 0, 0) * (1.0 / SAMPLES) for i in range(K)
        ]
        for p, (i, j) in enumerate(CROSS):
            at = (j - i) * BLK
            out[r, pl.ds(p * BLK, BLK), :] = scaled[i][:, at : at + BLK].astype(BF16)
        own = [block[:, :BLK] for block in scaled]
        out[r, pl.ds(3 * BLK, BLK), :] = own[2].astype(BF16)
        out[r, pl.ds(MIXED, BLK), :] = jnp.where(row <= col, own[0], own[1]).astype(BF16)
        lines = jnp.zeros((16, BLK), F32)
        for k in range(K):
            diag = jnp.sum(jnp.where(row == col, own[k], 0.0), axis=0, keepdims=True)
            high = diag.astype(BF16).astype(F32)
            lines = jnp.where(line == 2 * k, high, lines)
            lines = jnp.where(line == 2 * k + 1, diag - high, lines)
        out[r, pl.ds(DIAGS, 16), :] = lines.astype(BF16)
        return carry

    lax.fori_loop(0, ROWB, one, 0, unroll=True)


def on_strips(kernel, shape, specs, *args):
    arrays = args[len(specs) :]
    samples, columns = arrays[0].shape
    flops = 2 * ROWB * 6 * BLK * BLK * samples
    return pl.pallas_call(
        kernel,
        out_shape=jax.ShapeDtypeStruct(shape, BF16),
        in_specs=specs + [ANY] * len(arrays),
        out_specs=VMEM,
        scratch_shapes=[
            pltpu.VMEM((5, samples, columns), BF16),
            pltpu.SemaphoreType.DMA((len(arrays),)),
        ],
        compiler_params=params(),
        cost_estimate=pl.CostEstimate(flops=flops, bytes_accessed=12 * samples * columns, transcendentals=0),
        name=kernel.__name__,
    )(*args)


def times_gram(packed, high, low):
    total = jnp.zeros((BLK, K * BLK), F32)
    for j in range(K):
        rows = slice(j * BLK, (j + 1) * BLK)
        total += jnp.dot(packed[j], high[rows, :], preferred_element_type=F32)
        total += jnp.dot(packed[j], low[rows, :], preferred_element_type=F32)
    return [total[:, k * BLK : (k + 1) * BLK] for k in range(K)]


def put_squares(grads, out):
    squares = sum(jnp.sum(g * g, axis=0, keepdims=True) for g in grads)
    out[...] = jnp.broadcast_to(squares, out.shape)


def first_kernel(parts, omega, high, low, grad, squares):
    def summed(start, count):
        return sum(parts[s, pl.ds(start, count), :].astype(F32) for s in range(SAMP))

    def put(i, j, block):
        at = (pl.ds(i * BLK, BLK), pl.ds(j * BLK, BLK))
        top = block.astype(BF16)
        high[at] = top
        low[at] = (block - top.astype(F32)).astype(BF16)

    row, col = diagonal_mask()
    lines = summed(DIAGS, 16)
    mixed = summed(MIXED, BLK)
    flipped = mixed.T
    own = (
        jnp.where(row < col, mixed, flipped),
        jnp.where(row > col, mixed, flipped),
        summed(3 * BLK, BLK),
    )
    for k in range(K):
        diag = lines[2 * k : 2 * k + 1, :] + lines[2 * k + 1 : 2 * k + 2, :]
        put(k, k, jnp.where(row == col, diag, own[k]))
    for p, (i, j) in enumerate(CROSS):
        block = summed(p * BLK, BLK)
        put(i, j, block)
        put(j, i, block.T)
    grads = times_gram(omega, high, low)
    for k in range(K):
        grad[k] = grads[k]
    put_squares(grads, squares)


def step_of(squares):
    mean_sq = jnp.sum(squares[...]) * (1.0 / ENTRIES)
    mean_sq = jnp.full((8, BLK), mean_sq, F32)
    return (STEP_SCALE / jnp.sqrt(mean_sq + EPSILON))[0:1, :]


def proximal(iterate, grad, step, k):
    stepped = iterate - step * grad
    shrunk = stepped - jnp.clip(stepped, -THRESHOLD, THRESHOLD)
    if k:
        return shrunk
    row, col = diagonal_mask()
    barrier = 0.5 * (stepped + jnp.sqrt(stepped * stepped + 4.0 * step))
    return jnp.where(row == col, barrier, shrunk)


def second_kernel(squares, omega, grad, high, low, iterate, grad2, squares2):
    step = step_of(squares)
    packed = []
    for k in range(K):
        value = proximal(omega[k].astype(F32), grad[k], step, k)
        iterate[k] = value
        packed.append(value.astype(BF16))
    grads = times_gram(packed, high, low)
    for k in range(K):
        grad2[k] = grads[k]
    put_squares(grads, squares2)


def last_kernel(squares, iterate, grad, out):
    step = step_of(squares)
    for k in range(K):
        out[k] = proximal(iterate[k], grad[k], step, k)


def relay_kernel(rows, out):
    out[...] = jnp.broadcast_to(jnp.sum(rows[...], axis=0, keepdims=True), out.shape)


def call(kernel, shapes, *args):
    shapes = [jax.ShapeDtypeStruct(s, d) for s, d in shapes]
    return pl.pallas_call(
        kernel,
        out_shape=shapes,
        in_specs=[VMEM] * len(args),
        out_specs=[VMEM] * len(shapes),
        compiler_params=params(),
        name=kernel.__name__,
    )(*args)


def everywhere(rows):
    rows = lax.all_to_all(rows, ("xh", "y", "xl"), 0, 0, tiled=True)
    (rows,) = call(relay_kernel, [((32, BLK), F32)], rows)
    return lax.all_to_all(rows, ("z", "core"), 0, 0, tiled=True)


def swap(block, axis):
    return lax.ppermute(block, axis, [(0, 1), (1, 0)])


def along_z(block):
    depth, wide = SIZES[0], SIZES[1]
    route = []
    for z in range(depth):
        route.append((z * wide, (z + 1) % depth * wide))
        route.append((z * wide + 1, (z - 1) % depth * wide + 1))
    return lax.ppermute(block, ("z", "xh"), route)


def body(observed, pattern, omega_init):
    z, xh, core = (lax.axis_index(a) for a in VAR_AXES)
    samp = lax.axis_index("y") * 2 + lax.axis_index("xl")
    var = (z * 2 + xh) * 2 + core
    var_count = SIZES[0] * 4
    offset = (pattern // ROWB - var + var_count + 2) % var_count - 2
    near = jnp.where((offset == 1) == (core == 0), 1, 3)
    far = jnp.where((offset == 2) == (xh == 0), 2, 4)
    source = jnp.where(offset == 0, 0, jnp.where(abs(offset) == 1, near, far)).astype(jnp.int32)
    column = (pattern % ROWB).astype(jnp.int32)

    partner = swap(observed, "core")
    edges = [sum(SIZES_OF_CHUNKS[:i]) for i in range(CHUNKS + 1)]
    across = [swap(observed[a:b], "xh") for a, b in zip(edges, edges[1:])]
    beyond = [along_z(a) for a in across]
    beside = [swap(jnp.where(core == xh, a, b), "core") for a, b in zip(across, beyond)]
    strips = [observed, partner, *across, *beside, *beyond]
    grams = on_strips(gram_kernel, (ROWB, GRAM_ROWS, BLK), [SMEM, SMEM], source, column, *strips)
    parts = lax.all_to_all(grams, SAMP_AXES, 0, 0, tiled=True)
    omega = lax.dynamic_index_in_dim(omega_init, samp, 0, keepdims=False)
    side = K * BLK
    blocks = (K, BLK, BLK)
    high, low, grad, squares = call(
        first_kernel,
        [((side, side), BF16), ((side, side), BF16), (blocks, F32), ((16, BLK), F32)],
        parts,
        omega,
    )
    iterate, grad, squares = call(
        second_kernel,
        [(blocks, F32), (blocks, F32), ((16, BLK), F32)],
        everywhere(squares),
        omega,
        grad,
        high,
        low,
    )
    (precision,) = call(last_kernel, [(blocks, F32)], everywhere(squares), iterate, grad)
    return precision[None]


def solution(mesh):
    fine = Mesh(mesh.devices.reshape(SIZES), AXES)
    return jax.shard_map(
        body,
        mesh=fine,
        in_specs=(P(SAMP_AXES, VAR_AXES), P(VAR_AXES, None), P(VAR_AXES, None, None, None)),
        out_specs=P(AXES, None, None, None),
        check_vma=False,
    )
```

```python
import jax
import jax.numpy as jnp
from jax import lax
from jax.experimental import pallas as pl
from jax.experimental.pallas import tpu as pltpu
from jax.sharding import Mesh, PartitionSpec as P

STEP_SCALE = 0.5
THRESHOLD = 0.25
EPSILON = 1e-06

AXES = ("z", "xh", "core", "y", "xl")
SIZES = (16, 2, 2, 4, 2)
VAR_AXES = ("z", "xh", "core")
SAMP_AXES = ("y", "xl")
SIZES_OF_CHUNKS = (128, 128, 128, 128)
CHUNKS = len(SIZES_OF_CHUNKS)
ROWB = 8
K = 3
BLK = 128
SAMPLES = 4096
ENTRIES = 25165824
SAMP = 8
CROSS = ((0, 1), (0, 2), (1, 2))
HALF = BLK // 2
MIXED = 3 * BLK
FOLDED = 4 * BLK
DIAGS = FOLDED + HALF
GRAM_ROWS = DIAGS + 16

VMEM = pl.BlockSpec(memory_space=pltpu.VMEM)
SMEM = pl.BlockSpec(memory_space=pltpu.SMEM)
ANY = pl.BlockSpec(memory_space=pl.ANY)
F32 = jnp.float32
BF16 = jnp.bfloat16


def params():
    return pltpu.CompilerParams(vmem_limit_bytes=16 * 1024 * 1024)


def fetch(inputs, held, sems):
    copies = [pltpu.make_async_copy(inputs[i], held.at[i], sems.at[i]) for i in range(2)]
    for i in range(3 * CHUNKS):
        slot, chunk = 2 + i // CHUNKS, i % CHUNKS
        rows = pl.ds(sum(SIZES_OF_CHUNKS[:chunk]), SIZES_OF_CHUNKS[chunk])
        copies.append(pltpu.make_async_copy(inputs[2 + i], held.at[slot, rows], sems.at[2 + i]))
    for copy in copies:
        copy.start()
    for copy in copies:
        copy.wait()


def columns_of(held, source, column, r):
    return [
        held[source[r, k], :, pl.ds(pl.multiple_of(column[r, k] * BLK, BLK), BLK)] for k in range(K)
    ]


def dot(left, right, left_dim, right_dim):
    return lax.dot_general(
        left, right, (((left_dim,), (right_dim,)), ((), ())), preferred_element_type=F32
    )


def diagonal_mask():
    row = lax.broadcasted_iota(jnp.int32, (BLK, BLK), 0)
    col = lax.broadcasted_iota(jnp.int32, (BLK, BLK), 1)
    return row, col


def gram_kernel(source, column, *refs):
    *inputs, out, held, sems = refs
    fetch(inputs, held, sems)
    row, col = diagonal_mask()
    line = lax.broadcasted_iota(jnp.int32, (16, BLK), 0)

    def one(r, carry):
        cols = columns_of(held, source, column, r)
        scaled = [
            dot(cols[i], jnp.concatenate(cols[i:], axis=1), 0, 0) * (1.0 / SAMPLES) for i in range(K)
        ]
        for p, (i, j) in enumerate(CROSS):
            at = (j - i) * BLK
            out[r, pl.ds(p * BLK, BLK), :] = scaled[i][:, at : at + BLK].astype(BF16)
        own = [block[:, :BLK] for block in scaled]
        top, bottom = own[2][:HALF], pltpu.roll(own[2][HALF:], HALF, 1)
        folded = jnp.where(row[:HALF] <= col[:HALF], top, bottom)
        out[r, pl.ds(FOLDED, HALF), :] = folded.astype(BF16)
        out[r, pl.ds(MIXED, BLK), :] = jnp.where(row <= col, own[0], own[1]).astype(BF16)
        lines = jnp.zeros((16, BLK), F32)
        for k in range(K):
            diag = jnp.sum(jnp.where(row == col, own[k], 0.0), axis=0, keepdims=True)
            high = diag.astype(BF16).astype(F32)
            lines = jnp.where(line == 2 * k, high, lines)
            lines = jnp.where(line == 2 * k + 1, diag - high, lines)
        out[r, pl.ds(DIAGS, 16), :] = lines.astype(BF16)
        return carry

    lax.fori_loop(0, ROWB, one, 0, unroll=True)


def on_strips(kernel, shape, specs, *args):
    arrays = args[len(specs) :]
    samples, columns = arrays[0].shape
    flops = 2 * ROWB * 6 * BLK * BLK * samples
    return pl.pallas_call(
        kernel,
        out_shape=jax.ShapeDtypeStruct(shape, BF16),
        in_specs=specs + [ANY] * len(arrays),
        out_specs=VMEM,
        scratch_shapes=[
            pltpu.VMEM((5, samples, columns), BF16),
            pltpu.SemaphoreType.DMA((len(arrays),)),
        ],
        compiler_params=params(),
        cost_estimate=pl.CostEstimate(flops=flops, bytes_accessed=12 * samples * columns, transcendentals=0),
        name=kernel.__name__,
    )(*args)


def times_gram(packed, high, low):
    total = jnp.zeros((BLK, K * BLK), F32)
    for j in range(K):
        rows = slice(j * BLK, (j + 1) * BLK)
        total += jnp.dot(packed[j], high[rows, :], preferred_element_type=F32)
        total += jnp.dot(packed[j], low[rows, :], preferred_element_type=F32)
    return [total[:, k * BLK : (k + 1) * BLK] for k in range(K)]


def put_squares(grads, out):
    squares = sum(jnp.sum(g * g, axis=0, keepdims=True) for g in grads)
    out[...] = jnp.broadcast_to(squares, out.shape)


def first_kernel(parts, omega, high, low, grad, squares):
    def summed(start, count):
        return sum(parts[s, pl.ds(start, count), :].astype(F32) for s in range(SAMP))

    def put(i, j, block):
        at = (pl.ds(i * BLK, BLK), pl.ds(j * BLK, BLK))
        top = block.astype(BF16)
        high[at] = top
        low[at] = (block - top.astype(F32)).astype(BF16)

    row, col = diagonal_mask()
    lines = summed(DIAGS, 16)
    mixed = summed(MIXED, BLK)
    flipped = mixed.T
    folded = summed(FOLDED, HALF)
    unfolded = jnp.concatenate([folded, pltpu.roll(folded, HALF, 1)], axis=0)
    kept = ((row < HALF) & (row < col)) | ((col >= HALF) & (row > col))
    own = (
        jnp.where(row < col, mixed, flipped),
        jnp.where(row > col, mixed, flipped),
        jnp.where(kept, unfolded, unfolded.T),
    )
    for k in range(K):
        diag = lines[2 * k : 2 * k + 1, :] + lines[2 * k + 1 : 2 * k + 2, :]
        put(k, k, jnp.where(row == col, diag, own[k]))
    for p, (i, j) in enumerate(CROSS):
        block = summed(p * BLK, BLK)
        put(i, j, block)
        put(j, i, block.T)
    grads = times_gram(omega, high, low)
    for k in range(K):
        grad[k] = grads[k]
    put_squares(grads, squares)


def step_of(squares):
    mean_sq = jnp.sum(squares[...]) * (1.0 / ENTRIES)
    mean_sq = jnp.full((8, BLK), mean_sq, F32)
    return (STEP_SCALE / jnp.sqrt(mean_sq + EPSILON))[0:1, :]


def proximal(iterate, grad, step, k):
    stepped = iterate - step * grad
    shrunk = stepped - jnp.clip(stepped, -THRESHOLD, THRESHOLD)
    if k:
        return shrunk
    row, col = diagonal_mask()
    barrier = 0.5 * (stepped + jnp.sqrt(stepped * stepped + 4.0 * step))
    return jnp.where(row == col, barrier, shrunk)


def second_kernel(squares, omega, grad, high, low, iterate, grad2, squares2):
    step = step_of(squares)
    packed = []
    for k in range(K):
        value = proximal(omega[k].astype(F32), grad[k], step, k)
        iterate[k] = value
        packed.append(value.astype(BF16))
    grads = times_gram(packed, high, low)
    for k in range(K):
        grad2[k] = grads[k]
    put_squares(grads, squares2)


def last_kernel(squares, iterate, grad, out):
    step = step_of(squares)
    for k in range(K):
        out[k] = proximal(iterate[k], grad[k], step, k)


def relay_kernel(rows, out):
    out[...] = jnp.broadcast_to(jnp.sum(rows[...], axis=0, keepdims=True), out.shape)


def call(kernel, shapes, *args):
    shapes = [jax.ShapeDtypeStruct(s, d) for s, d in shapes]
    return pl.pallas_call(
        kernel,
        out_shape=shapes,
        in_specs=[VMEM] * len(args),
        out_specs=[VMEM] * len(shapes),
        compiler_params=params(),
        name=kernel.__name__,
    )(*args)


def everywhere(rows):
    rows = lax.all_to_all(rows, ("xh", "y", "xl"), 0, 0, tiled=True)
    (rows,) = call(relay_kernel, [((32, BLK), F32)], rows)
    return lax.all_to_all(rows, ("z", "core"), 0, 0, tiled=True)


def swap(block, axis):
    return lax.ppermute(block, axis, [(0, 1), (1, 0)])


def along_z(block):
    depth, wide = SIZES[0], SIZES[1]
    route = []
    for z in range(depth):
        route.append((z * wide, (z + 1) % depth * wide))
        route.append((z * wide + 1, (z - 1) % depth * wide + 1))
    return lax.ppermute(block, ("z", "xh"), route)


def body(observed, pattern, omega_init):
    z, xh, core = (lax.axis_index(a) for a in VAR_AXES)
    samp = lax.axis_index("y") * 2 + lax.axis_index("xl")
    var = (z * 2 + xh) * 2 + core
    var_count = SIZES[0] * 4
    offset = (pattern // ROWB - var + var_count + 2) % var_count - 2
    near = jnp.where((offset == 1) == (core == 0), 1, 3)
    far = jnp.where((offset == 2) == (xh == 0), 2, 4)
    source = jnp.where(offset == 0, 0, jnp.where(abs(offset) == 1, near, far)).astype(jnp.int32)
    column = (pattern % ROWB).astype(jnp.int32)

    partner = swap(observed, "core")
    edges = [sum(SIZES_OF_CHUNKS[:i]) for i in range(CHUNKS + 1)]
    across = [swap(observed[a:b], "xh") for a, b in zip(edges, edges[1:])]
    beyond = [along_z(a) for a in across]
    beside = [swap(jnp.where(core == xh, a, b), "core") for a, b in zip(across, beyond)]
    strips = [observed, partner, *across, *beside, *beyond]
    grams = on_strips(gram_kernel, (ROWB, GRAM_ROWS, BLK), [SMEM, SMEM], source, column, *strips)
    parts = lax.all_to_all(grams, SAMP_AXES, 0, 0, tiled=True)
    omega = lax.dynamic_index_in_dim(omega_init, samp, 0, keepdims=False)
    side = K * BLK
    blocks = (K, BLK, BLK)
    high, low, grad, squares = call(
        first_kernel,
        [((side, side), BF16), ((side, side), BF16), (blocks, F32), ((16, BLK), F32)],
        parts,
        omega,
    )
    iterate, grad, squares = call(
        second_kernel,
        [(blocks, F32), (blocks, F32), ((16, BLK), F32)],
        everywhere(squares),
        omega,
        grad,
        high,
        low,
    )
    (precision,) = call(last_kernel, [(blocks, F32)], everywhere(squares), iterate, grad)
    return precision[None]


def solution(mesh):
    fine = Mesh(mesh.devices.reshape(SIZES), AXES)
    return jax.shard_map(
        body,
        mesh=fine,
        in_specs=(P(SAMP_AXES, VAR_AXES), P(VAR_AXES, None), P(VAR_AXES, None, None, None)),
        out_specs=P(AXES, None, None, None),
        check_vma=False,
    )
```

```python
import jax
import jax.numpy as jnp
from jax import lax
from jax.experimental import pallas as pl
from jax.experimental.pallas import tpu as pltpu
from jax.sharding import Mesh, PartitionSpec as P

STEP_SCALE = 0.5
THRESHOLD = 0.25
EPSILON = 1e-06

AXES = ("z", "xh", "core", "y", "xl")
SIZES = (16, 2, 2, 4, 2)
VAR_AXES = ("z", "xh", "core")
SAMP_AXES = ("y", "xl")
SIZES_OF_CHUNKS = (176, 176, 160)
CHUNKS = len(SIZES_OF_CHUNKS)
ROWB = 8
K = 3
BLK = 128
SAMPLES = 4096
ENTRIES = 25165824
SAMP = 8
CROSS = ((0, 1), (0, 2), (1, 2))
HALF = BLK // 2
MIXED = 3 * BLK
FOLDED = 4 * BLK
DIAGS = FOLDED + HALF
GRAM_ROWS = DIAGS + 16

VMEM = pl.BlockSpec(memory_space=pltpu.VMEM)
SMEM = pl.BlockSpec(memory_space=pltpu.SMEM)
ANY = pl.BlockSpec(memory_space=pl.ANY)
F32 = jnp.float32
BF16 = jnp.bfloat16


def params():
    return pltpu.CompilerParams(vmem_limit_bytes=16 * 1024 * 1024)


def choose(inputs, held, source, column):
    def one(n, carry):
        r, k = n // (K - 1), n % (K - 1) + 1
        at = pl.ds(pl.multiple_of(column[r, k] * BLK, BLK), BLK)
        for slot in range(1, 5):

            @pl.when(source[r, k] == slot)
            def _():
                start = 0
                for strip in inputs[slot]:
                    rows = strip.shape[0]
                    held[n, pl.ds(start, rows), :] = strip[:, at]
                    start += rows

        return carry

    lax.fori_loop(0, ROWB * (K - 1), one, 0)


def dot(left, right, left_dim, right_dim):
    return lax.dot_general(
        left, right, (((left_dim,), (right_dim,)), ((), ())), preferred_element_type=F32
    )


def diagonal_mask():
    row = lax.broadcasted_iota(jnp.int32, (BLK, BLK), 0)
    col = lax.broadcasted_iota(jnp.int32, (BLK, BLK), 1)
    return row, col


def gram_kernel(source, column, *refs):
    *strips, out, held = refs
    inputs = [strips[:1], strips[1:2]]
    inputs += [strips[2 + CHUNKS * i : 2 + CHUNKS * (i + 1)] for i in range(3)]
    choose(inputs, held, source, column)
    row, col = diagonal_mask()
    line = lax.broadcasted_iota(jnp.int32, (16, BLK), 0)

    for r in range(ROWB):
        cols = [strips[0][:, r * BLK : (r + 1) * BLK], held[2 * r], held[2 * r + 1]]
        scaled = [
            dot(cols[i], jnp.concatenate(cols[i:], axis=1), 0, 0) * (1.0 / SAMPLES) for i in range(K)
        ]
        for p, (i, j) in enumerate(CROSS):
            at = (j - i) * BLK
            out[r, pl.ds(p * BLK, BLK), :] = scaled[i][:, at : at + BLK].astype(BF16)
        own = [block[:, :BLK] for block in scaled]
        top, bottom = own[2][:HALF], pltpu.roll(own[2][HALF:], HALF, 1)
        folded = jnp.where(row[:HALF] <= col[:HALF], top, bottom)
        out[r, pl.ds(FOLDED, HALF), :] = folded.astype(BF16)
        out[r, pl.ds(MIXED, BLK), :] = jnp.where(row <= col, own[0], own[1]).astype(BF16)
        lines = jnp.zeros((16, BLK), F32)
        for k in range(K):
            diag = jnp.sum(jnp.where(row == col, own[k], 0.0), axis=0, keepdims=True)
            high = diag.astype(BF16).astype(F32)
            lines = jnp.where(line == 2 * k, high, lines)
            lines = jnp.where(line == 2 * k + 1, diag - high, lines)
        out[r, pl.ds(DIAGS, 16), :] = lines.astype(BF16)


def on_strips(kernel, shape, specs, *args):
    arrays = args[len(specs) :]
    samples, columns = arrays[0].shape
    flops = 2 * ROWB * 6 * BLK * BLK * samples
    return pl.pallas_call(
        kernel,
        out_shape=jax.ShapeDtypeStruct(shape, BF16),
        in_specs=specs + [VMEM] * len(arrays),
        out_specs=VMEM,
        scratch_shapes=[pltpu.VMEM((ROWB * (K - 1), samples, BLK), BF16)],
        compiler_params=params(),
        cost_estimate=pl.CostEstimate(flops=flops, bytes_accessed=12 * samples * columns, transcendentals=0),
        name=kernel.__name__,
    )(*args)


def times_gram(packed, high, low):
    total = jnp.zeros((BLK, K * BLK), F32)
    for j in range(K):
        rows = slice(j * BLK, (j + 1) * BLK)
        total += jnp.dot(packed[j], high[rows, :], preferred_element_type=F32)
        total += jnp.dot(packed[j], low[rows, :], preferred_element_type=F32)
    return [total[:, k * BLK : (k + 1) * BLK] for k in range(K)]


def put_squares(grads, out):
    squares = sum(jnp.sum(g * g, axis=0, keepdims=True) for g in grads)
    out[...] = jnp.broadcast_to(squares, out.shape)


def first_kernel(parts, omega, high, low, grad, squares):
    def summed(start, count):
        return sum(parts[s, pl.ds(start, count), :].astype(F32) for s in range(SAMP))

    def put(i, j, block):
        at = (pl.ds(i * BLK, BLK), pl.ds(j * BLK, BLK))
        top = block.astype(BF16)
        high[at] = top
        low[at] = (block - top.astype(F32)).astype(BF16)

    row, col = diagonal_mask()
    lines = summed(DIAGS, 16)
    mixed = summed(MIXED, BLK)
    flipped = mixed.T
    folded = summed(FOLDED, HALF)
    unfolded = jnp.concatenate([folded, pltpu.roll(folded, HALF, 1)], axis=0)
    kept = ((row < HALF) & (row < col)) | ((col >= HALF) & (row > col))
    own = (
        jnp.where(row < col, mixed, flipped),
        jnp.where(row > col, mixed, flipped),
        jnp.where(kept, unfolded, unfolded.T),
    )
    for k in range(K):
        diag = lines[2 * k : 2 * k + 1, :] + lines[2 * k + 1 : 2 * k + 2, :]
        put(k, k, jnp.where(row == col, diag, own[k]))
    for p, (i, j) in enumerate(CROSS):
        block = summed(p * BLK, BLK)
        put(i, j, block)
        put(j, i, block.T)
    grads = times_gram(omega, high, low)
    for k in range(K):
        grad[k] = grads[k]
    put_squares(grads, squares)


def step_of(squares):
    mean_sq = jnp.sum(squares[...]) * (1.0 / ENTRIES)
    mean_sq = jnp.full((8, BLK), mean_sq, F32)
    return (STEP_SCALE / jnp.sqrt(mean_sq + EPSILON))[0:1, :]


def proximal(iterate, grad, step, k):
    stepped = iterate - step * grad
    shrunk = stepped - jnp.clip(stepped, -THRESHOLD, THRESHOLD)
    if k:
        return shrunk
    row, col = diagonal_mask()
    barrier = 0.5 * (stepped + jnp.sqrt(stepped * stepped + 4.0 * step))
    return jnp.where(row == col, barrier, shrunk)


def second_kernel(squares, omega, grad, high, low, iterate, grad2, squares2):
    step = step_of(squares)
    packed = []
    for k in range(K):
        value = proximal(omega[k].astype(F32), grad[k], step, k)
        iterate[k] = value
        packed.append(value.astype(BF16))
    grads = times_gram(packed, high, low)
    for k in range(K):
        grad2[k] = grads[k]
    put_squares(grads, squares2)


def last_kernel(squares, iterate, grad, out):
    step = step_of(squares)
    for k in range(K):
        out[k] = proximal(iterate[k], grad[k], step, k)


def relay_kernel(rows, out):
    out[...] = jnp.broadcast_to(jnp.sum(rows[...], axis=0, keepdims=True), out.shape)


def call(kernel, shapes, *args):
    shapes = [jax.ShapeDtypeStruct(s, d) for s, d in shapes]
    return pl.pallas_call(
        kernel,
        out_shape=shapes,
        in_specs=[VMEM] * len(args),
        out_specs=[VMEM] * len(shapes),
        compiler_params=params(),
        name=kernel.__name__,
    )(*args)


def everywhere(rows):
    rows = lax.all_to_all(rows, ("xh", "y", "xl"), 0, 0, tiled=True)
    (rows,) = call(relay_kernel, [((32, BLK), F32)], rows)
    return lax.all_to_all(rows, ("z", "core"), 0, 0, tiled=True)


def swap(block, axis):
    return lax.ppermute(block, axis, [(0, 1), (1, 0)])


def along_z(block):
    depth, wide = SIZES[0], SIZES[1]
    route = []
    for z in range(depth):
        route.append((z * wide, (z + 1) % depth * wide))
        route.append((z * wide + 1, (z - 1) % depth * wide + 1))
    return lax.ppermute(block, ("z", "xh"), route)


def body(observed, pattern, omega_init):
    z, xh, core = (lax.axis_index(a) for a in VAR_AXES)
    samp = lax.axis_index("y") * 2 + lax.axis_index("xl")
    var = (z * 2 + xh) * 2 + core
    var_count = SIZES[0] * 4
    offset = (pattern // ROWB - var + var_count + 2) % var_count - 2
    near = jnp.where((offset == 1) == (core == 0), 1, 3)
    far = jnp.where((offset == 2) == (xh == 0), 2, 4)
    source = jnp.where(offset == 0, 0, jnp.where(abs(offset) == 1, near, far)).astype(jnp.int32)
    column = (pattern % ROWB).astype(jnp.int32)

    partner = swap(observed, "core")
    edges = [sum(SIZES_OF_CHUNKS[:i]) for i in range(CHUNKS + 1)]
    across = [swap(observed[a:b], "xh") for a, b in zip(edges, edges[1:])]
    beyond = [along_z(a) for a in across]
    beside = [swap(jnp.where(core == xh, a, b), "core") for a, b in zip(across, beyond)]
    strips = [observed, partner, *across, *beside, *beyond]
    grams = on_strips(gram_kernel, (ROWB, GRAM_ROWS, BLK), [SMEM, SMEM], source, column, *strips)
    parts = lax.all_to_all(grams, SAMP_AXES, 0, 0, tiled=True)
    omega = lax.dynamic_index_in_dim(omega_init, samp, 0, keepdims=False)
    side = K * BLK
    blocks = (K, BLK, BLK)
    high, low, grad, squares = call(
        first_kernel,
        [((side, side), BF16), ((side, side), BF16), (blocks, F32), ((16, BLK), F32)],
        parts,
        omega,
    )
    iterate, grad, squares = call(
        second_kernel,
        [(blocks, F32), (blocks, F32), ((16, BLK), F32)],
        everywhere(squares),
        omega,
        grad,
        high,
        low,
    )
    (precision,) = call(last_kernel, [(blocks, F32)], everywhere(squares), iterate, grad)
    return precision[None]


def solution(mesh):
    fine = Mesh(mesh.devices.reshape(SIZES), AXES)
    return jax.shard_map(
        body,
        mesh=fine,
        in_specs=(P(SAMP_AXES, VAR_AXES), P(VAR_AXES, None), P(VAR_AXES, None, None, None)),
        out_specs=P(AXES, None, None, None),
        check_vma=False,
    )
```

```python
import jax
import jax.numpy as jnp
from jax import lax
from jax.experimental import pallas as pl
from jax.experimental.pallas import tpu as pltpu
from jax.sharding import Mesh, PartitionSpec as P

STEP_SCALE = 0.5
THRESHOLD = 0.25
EPSILON = 1e-06

AXES = ("z", "xh", "core", "y", "xl")
SIZES = (16, 2, 2, 4, 2)
VAR_AXES = ("z", "xh", "core")
SAMP_AXES = ("y", "xl")
SIZES_OF_CHUNKS = (176, 176, 160)
CHUNKS = len(SIZES_OF_CHUNKS)
ROWB = 8
K = 3
BLK = 128
SAMPLES = 4096
ENTRIES = 25165824
SAMP = 8
CROSS = ((0, 1), (0, 2), (1, 2))
HALF = BLK // 2
MIXED = 3 * BLK
FOLDED = 4 * BLK
DIAGS = FOLDED + HALF
GRAM_ROWS = DIAGS + 16

VMEM = pl.BlockSpec(memory_space=pltpu.VMEM)
SMEM = pl.BlockSpec(memory_space=pltpu.SMEM)
ANY = pl.BlockSpec(memory_space=pl.ANY)
F32 = jnp.float32
BF16 = jnp.bfloat16


def params():
    return pltpu.CompilerParams(vmem_limit_bytes=16 * 1024 * 1024)


STRIPS = (
    (0, 1),
    (1, 2),
    (2, 2 + CHUNKS),
    (2 + CHUNKS, 3 + 2 * CHUNKS),
    (3 + 2 * CHUNKS, 3 + 3 * CHUNKS),
)


def choose(inputs, held, source, column):
    def one(n, carry):
        r, k = n // (K - 1), n % (K - 1) + 1
        at = pl.ds(pl.multiple_of(column[r, k] * BLK, BLK), BLK)
        for slot in range(1, 5):

            @pl.when(source[r, k] == slot)
            def _():
                start = 0
                for strip in inputs[slot]:
                    rows = strip[0].shape[0]
                    held[n, pl.ds(start, rows), :] = sum(part[:, at] for part in strip)
                    start += rows

        return carry

    lax.fori_loop(0, ROWB * (K - 1), one, 0)


def dot(left, right, left_dim, right_dim):
    return lax.dot_general(
        left, right, (((left_dim,), (right_dim,)), ((), ())), preferred_element_type=F32
    )


def diagonal_mask():
    row = lax.broadcasted_iota(jnp.int32, (BLK, BLK), 0)
    col = lax.broadcasted_iota(jnp.int32, (BLK, BLK), 1)
    return row, col


def gram_kernel(source, column, *refs):
    *strips, out, held = refs
    inputs = [[(strip,) for strip in strips[a:b]] for a, b in STRIPS]
    inputs[3][-2:] = [inputs[3][-2] + inputs[3][-1]]
    choose(inputs, held, source, column)
    row, col = diagonal_mask()
    line = lax.broadcasted_iota(jnp.int32, (16, BLK), 0)

    for r in range(ROWB):
        cols = [strips[0][:, r * BLK : (r + 1) * BLK], held[2 * r], held[2 * r + 1]]
        scaled = [
            dot(cols[i], jnp.concatenate(cols[i:], axis=1), 0, 0) * (1.0 / SAMPLES) for i in range(K)
        ]
        for p, (i, j) in enumerate(CROSS):
            at = (j - i) * BLK
            out[r, pl.ds(p * BLK, BLK), :] = scaled[i][:, at : at + BLK].astype(BF16)
        own = [block[:, :BLK] for block in scaled]
        top, bottom = own[2][:HALF], pltpu.roll(own[2][HALF:], HALF, 1)
        folded = jnp.where(row[:HALF] <= col[:HALF], top, bottom)
        out[r, pl.ds(FOLDED, HALF), :] = folded.astype(BF16)
        out[r, pl.ds(MIXED, BLK), :] = jnp.where(row <= col, own[0], own[1]).astype(BF16)
        lines = jnp.zeros((16, BLK), F32)
        for k in range(K):
            diag = jnp.sum(jnp.where(row == col, own[k], 0.0), axis=0, keepdims=True)
            high = diag.astype(BF16).astype(F32)
            lines = jnp.where(line == 2 * k, high, lines)
            lines = jnp.where(line == 2 * k + 1, diag - high, lines)
        out[r, pl.ds(DIAGS, 16), :] = lines.astype(BF16)


def on_strips(kernel, shape, specs, *args):
    arrays = args[len(specs) :]
    samples, columns = arrays[0].shape
    flops = 2 * ROWB * 6 * BLK * BLK * samples
    return pl.pallas_call(
        kernel,
        out_shape=jax.ShapeDtypeStruct(shape, BF16),
        in_specs=specs + [VMEM] * len(arrays),
        out_specs=VMEM,
        scratch_shapes=[pltpu.VMEM((ROWB * (K - 1), samples, BLK), BF16)],
        compiler_params=params(),
        cost_estimate=pl.CostEstimate(flops=flops, bytes_accessed=12 * samples * columns, transcendentals=0),
        name=kernel.__name__,
    )(*args)


def times_gram(packed, high, low):
    total = jnp.zeros((BLK, K * BLK), F32)
    for j in range(K):
        rows = slice(j * BLK, (j + 1) * BLK)
        total += jnp.dot(packed[j], high[rows, :], preferred_element_type=F32)
        total += jnp.dot(packed[j], low[rows, :], preferred_element_type=F32)
    return [total[:, k * BLK : (k + 1) * BLK] for k in range(K)]


def put_squares(grads, out):
    squares = sum(jnp.sum(g * g, axis=0, keepdims=True) for g in grads)
    out[...] = jnp.broadcast_to(squares, out.shape)


def first_kernel(parts, omega, high, low, grad, squares):
    def summed(start, count):
        return sum(parts[s, pl.ds(start, count), :].astype(F32) for s in range(SAMP))

    def put(i, j, block):
        at = (pl.ds(i * BLK, BLK), pl.ds(j * BLK, BLK))
        top = block.astype(BF16)
        high[at] = top
        low[at] = (block - top.astype(F32)).astype(BF16)

    row, col = diagonal_mask()
    lines = summed(DIAGS, 16)
    mixed = summed(MIXED, BLK)
    flipped = mixed.T
    folded = summed(FOLDED, HALF)
    unfolded = jnp.concatenate([folded, pltpu.roll(folded, HALF, 1)], axis=0)
    kept = ((row < HALF) & (row < col)) | ((col >= HALF) & (row > col))
    own = (
        jnp.where(row < col, mixed, flipped),
        jnp.where(row > col, mixed, flipped),
        jnp.where(kept, unfolded, unfolded.T),
    )
    for k in range(K):
        diag = lines[2 * k : 2 * k + 1, :] + lines[2 * k + 1 : 2 * k + 2, :]
        put(k, k, jnp.where(row == col, diag, own[k]))
    for p, (i, j) in enumerate(CROSS):
        block = summed(p * BLK, BLK)
        put(i, j, block)
        put(j, i, block.T)
    grads = times_gram(omega, high, low)
    for k in range(K):
        grad[k] = grads[k]
    put_squares(grads, squares)


def step_of(squares):
    mean_sq = jnp.sum(squares[...]) * (1.0 / ENTRIES)
    mean_sq = jnp.full((8, BLK), mean_sq, F32)
    return (STEP_SCALE / jnp.sqrt(mean_sq + EPSILON))[0:1, :]


def proximal(iterate, grad, step, k):
    stepped = iterate - step * grad
    shrunk = stepped - jnp.clip(stepped, -THRESHOLD, THRESHOLD)
    if k:
        return shrunk
    row, col = diagonal_mask()
    barrier = 0.5 * (stepped + jnp.sqrt(stepped * stepped + 4.0 * step))
    return jnp.where(row == col, barrier, shrunk)


def second_kernel(squares, omega, grad, high, low, iterate, grad2, squares2):
    step = step_of(squares)
    packed = []
    for k in range(K):
        value = proximal(omega[k].astype(F32), grad[k], step, k)
        iterate[k] = value
        packed.append(value.astype(BF16))
    grads = times_gram(packed, high, low)
    for k in range(K):
        grad2[k] = grads[k]
    put_squares(grads, squares2)


def last_kernel(squares, iterate, grad, out):
    step = step_of(squares)
    for k in range(K):
        out[k] = proximal(iterate[k], grad[k], step, k)


def relay_kernel(rows, out):
    out[...] = jnp.broadcast_to(jnp.sum(rows[...], axis=0, keepdims=True), out.shape)


def call(kernel, shapes, *args):
    shapes = [jax.ShapeDtypeStruct(s, d) for s, d in shapes]
    return pl.pallas_call(
        kernel,
        out_shape=shapes,
        in_specs=[VMEM] * len(args),
        out_specs=[VMEM] * len(shapes),
        compiler_params=params(),
        name=kernel.__name__,
    )(*args)


def everywhere(rows):
    rows = lax.all_to_all(rows, ("xh", "y", "xl"), 0, 0, tiled=True)
    (rows,) = call(relay_kernel, [((32, BLK), F32)], rows)
    return lax.all_to_all(rows, ("z", "core"), 0, 0, tiled=True)


def swap(block, axis):
    return lax.ppermute(block, axis, [(0, 1), (1, 0)])


def swap_some(block, alike):
    route = [(0, 1), (3, 2)] if alike else [(1, 0), (2, 3)]
    return lax.ppermute(block, ("xh", "core"), route)


def along_z(block):
    depth, wide = SIZES[0], SIZES[1]
    route = []
    for z in range(depth):
        route.append((z * wide, (z + 1) % depth * wide))
        route.append((z * wide + 1, (z - 1) % depth * wide + 1))
    return lax.ppermute(block, ("z", "xh"), route)


def body(observed, pattern, omega_init):
    z, xh, core = (lax.axis_index(a) for a in VAR_AXES)
    samp = lax.axis_index("y") * 2 + lax.axis_index("xl")
    var = (z * 2 + xh) * 2 + core
    var_count = SIZES[0] * 4
    offset = (pattern // ROWB - var + var_count + 2) % var_count - 2
    near = jnp.where((offset == 1) == (core == 0), 1, 3)
    far = jnp.where((offset == 2) == (xh == 0), 2, 4)
    source = jnp.where(offset == 0, 0, jnp.where(abs(offset) == 1, near, far)).astype(jnp.int32)
    column = (pattern % ROWB).astype(jnp.int32)

    partner = swap(observed, "core")
    edges = [sum(SIZES_OF_CHUNKS[:i]) for i in range(CHUNKS + 1)]
    across = [swap(observed[a:b], "xh") for a, b in zip(edges, edges[1:])]
    beyond = [along_z(a) for a in across]
    beside = [swap(jnp.where(core == xh, a, b), "core") for a, b in zip(across[:-1], beyond[:-1])]
    beside += [swap_some(across[-1], True), swap_some(beyond[-1], False)]
    strips = [observed, partner, *across, *beside, *beyond]
    grams = on_strips(gram_kernel, (ROWB, GRAM_ROWS, BLK), [SMEM, SMEM], source, column, *strips)
    parts = lax.all_to_all(grams, SAMP_AXES, 0, 0, tiled=True)
    omega = lax.dynamic_index_in_dim(omega_init, samp, 0, keepdims=False)
    side = K * BLK
    blocks = (K, BLK, BLK)
    high, low, grad, squares = call(
        first_kernel,
        [((side, side), BF16), ((side, side), BF16), (blocks, F32), ((16, BLK), F32)],
        parts,
        omega,
    )
    iterate, grad, squares = call(
        second_kernel,
        [(blocks, F32), (blocks, F32), ((16, BLK), F32)],
        everywhere(squares),
        omega,
        grad,
        high,
        low,
    )
    (precision,) = call(last_kernel, [(blocks, F32)], everywhere(squares), iterate, grad)
    return precision[None]


def solution(mesh):
    fine = Mesh(mesh.devices.reshape(SIZES), AXES)
    return jax.shard_map(
        body,
        mesh=fine,
        in_specs=(P(SAMP_AXES, VAR_AXES), P(VAR_AXES, None), P(VAR_AXES, None, None, None)),
        out_specs=P(AXES, None, None, None),
        check_vma=False,
    )
```

```python
import jax
import jax.numpy as jnp
from jax import lax
from jax.experimental import pallas as pl
from jax.experimental.pallas import tpu as pltpu
from jax.sharding import Mesh, PartitionSpec as P

STEP_SCALE = 0.5
THRESHOLD = 0.25
EPSILON = 1e-06

AXES = ("z", "xh", "core", "y", "xl")
SIZES = (16, 2, 2, 4, 2)
VAR_AXES = ("z", "xh", "core")
SAMP_AXES = ("y", "xl")
SIZES_OF_CHUNKS = (192, 176, 144)
CHUNKS = len(SIZES_OF_CHUNKS)
ROWB = 8
K = 3
BLK = 128
SAMPLES = 4096
ENTRIES = 25165824
SAMP = 8
CROSS = ((0, 1), (0, 2), (1, 2))
HALF = BLK // 2
MIXED = 3 * BLK
FOLDED = 4 * BLK
DIAGS = FOLDED + HALF
GRAM_ROWS = DIAGS + 16

VMEM = pl.BlockSpec(memory_space=pltpu.VMEM)
SMEM = pl.BlockSpec(memory_space=pltpu.SMEM)
ANY = pl.BlockSpec(memory_space=pl.ANY)
F32 = jnp.float32
BF16 = jnp.bfloat16


def params():
    return pltpu.CompilerParams(vmem_limit_bytes=16 * 1024 * 1024)


STRIPS = (
    (0, 1),
    (1, 3),
    (3, 3 + CHUNKS),
    (3 + CHUNKS, 4 + 2 * CHUNKS),
    (4 + 2 * CHUNKS, 4 + 3 * CHUNKS),
)


def choose(inputs, held, source, column):
    def one(n, carry):
        r, k = n // (K - 1), n % (K - 1) + 1
        at = pl.ds(pl.multiple_of(column[r, k] * BLK, BLK), BLK)
        for slot in range(1, 5):

            @pl.when(source[r, k] == slot)
            def _():
                start = 0
                for strip in inputs[slot]:
                    rows = strip[0].shape[0]
                    held[n, pl.ds(start, rows), :] = sum(part[:, at] for part in strip)
                    start += rows

        return carry

    lax.fori_loop(0, ROWB * (K - 1), one, 0)


def dot(left, right, left_dim, right_dim):
    return lax.dot_general(
        left, right, (((left_dim,), (right_dim,)), ((), ())), preferred_element_type=F32
    )


def diagonal_mask():
    row = lax.broadcasted_iota(jnp.int32, (BLK, BLK), 0)
    col = lax.broadcasted_iota(jnp.int32, (BLK, BLK), 1)
    return row, col


def gram_kernel(source, column, *refs):
    *strips, out, held = refs
    inputs = [[(strip,) for strip in strips[a:b]] for a, b in STRIPS]
    inputs[3][-2:] = [inputs[3][-2] + inputs[3][-1]]
    choose(inputs, held, source, column)
    row, col = diagonal_mask()
    line = lax.broadcasted_iota(jnp.int32, (16, BLK), 0)

    for r in range(ROWB):
        cols = [strips[0][:, r * BLK : (r + 1) * BLK], held[2 * r], held[2 * r + 1]]
        scaled = [
            dot(cols[i], jnp.concatenate(cols[i:], axis=1), 0, 0) * (1.0 / SAMPLES) for i in range(K)
        ]
        for p, (i, j) in enumerate(CROSS):
            at = (j - i) * BLK
            out[r, pl.ds(p * BLK, BLK), :] = scaled[i][:, at : at + BLK].astype(BF16)
        own = [block[:, :BLK] for block in scaled]
        top, bottom = own[2][:HALF], pltpu.roll(own[2][HALF:], HALF, 1)
        folded = jnp.where(row[:HALF] <= col[:HALF], top, bottom)
        out[r, pl.ds(FOLDED, HALF), :] = folded.astype(BF16)
        out[r, pl.ds(MIXED, BLK), :] = jnp.where(row <= col, own[0], own[1]).astype(BF16)
        lines = jnp.zeros((16, BLK), F32)
        for k in range(K):
            diag = jnp.sum(jnp.where(row == col, own[k], 0.0), axis=0, keepdims=True)
            high = diag.astype(BF16).astype(F32)
            lines = jnp.where(line == 2 * k, high, lines)
            lines = jnp.where(line == 2 * k + 1, diag - high, lines)
        out[r, pl.ds(DIAGS, 16), :] = lines.astype(BF16)


def on_strips(kernel, shape, specs, *args):
    arrays = args[len(specs) :]
    samples, columns = arrays[0].shape
    flops = 2 * ROWB * 6 * BLK * BLK * samples
    return pl.pallas_call(
        kernel,
        out_shape=jax.ShapeDtypeStruct(shape, BF16),
        in_specs=specs + [VMEM] * len(arrays),
        out_specs=VMEM,
        scratch_shapes=[pltpu.VMEM((ROWB * (K - 1), samples, BLK), BF16)],
        compiler_params=params(),
        cost_estimate=pl.CostEstimate(flops=flops, bytes_accessed=12 * samples * columns, transcendentals=0),
        name=kernel.__name__,
    )(*args)


def times_gram(packed, high, low):
    total = jnp.zeros((BLK, K * BLK), F32)
    for j in range(K):
        rows = slice(j * BLK, (j + 1) * BLK)
        total += jnp.dot(packed[j], high[rows, :], preferred_element_type=F32)
        total += jnp.dot(packed[j], low[rows, :], preferred_element_type=F32)
    return [total[:, k * BLK : (k + 1) * BLK] for k in range(K)]


def put_squares(grads, out):
    squares = sum(jnp.sum(g * g, axis=0, keepdims=True) for g in grads)
    out[...] = jnp.broadcast_to(squares, out.shape)


def first_kernel(parts, omega, high, low, grad, squares):
    def summed(start, count):
        return sum(parts[s, pl.ds(start, count), :].astype(F32) for s in range(SAMP))

    def put(i, j, block):
        at = (pl.ds(i * BLK, BLK), pl.ds(j * BLK, BLK))
        top = block.astype(BF16)
        high[at] = top
        low[at] = (block - top.astype(F32)).astype(BF16)

    row, col = diagonal_mask()
    lines = summed(DIAGS, 16)
    mixed = summed(MIXED, BLK)
    flipped = mixed.T
    folded = summed(FOLDED, HALF)
    unfolded = jnp.concatenate([folded, pltpu.roll(folded, HALF, 1)], axis=0)
    kept = ((row < HALF) & (row < col)) | ((col >= HALF) & (row > col))
    own = (
        jnp.where(row < col, mixed, flipped),
        jnp.where(row > col, mixed, flipped),
        jnp.where(kept, unfolded, unfolded.T),
    )
    for k in range(K):
        diag = lines[2 * k : 2 * k + 1, :] + lines[2 * k + 1 : 2 * k + 2, :]
        put(k, k, jnp.where(row == col, diag, own[k]))
    for p, (i, j) in enumerate(CROSS):
        block = summed(p * BLK, BLK)
        put(i, j, block)
        put(j, i, block.T)
    grads = times_gram(omega, high, low)
    for k in range(K):
        grad[k] = grads[k]
    put_squares(grads, squares)


def step_of(squares):
    mean_sq = jnp.sum(squares[...]) * (1.0 / ENTRIES)
    mean_sq = jnp.full((8, BLK), mean_sq, F32)
    return (STEP_SCALE / jnp.sqrt(mean_sq + EPSILON))[0:1, :]


def proximal(iterate, grad, step, k):
    stepped = iterate - step * grad
    shrunk = stepped - jnp.clip(stepped, -THRESHOLD, THRESHOLD)
    if k:
        return shrunk
    row, col = diagonal_mask()
    barrier = 0.5 * (stepped + jnp.sqrt(stepped * stepped + 4.0 * step))
    return jnp.where(row == col, barrier, shrunk)


def second_kernel(squares, omega, grad, high, low, iterate, grad2, squares2):
    step = step_of(squares)
    packed = []
    for k in range(K):
        value = proximal(omega[k].astype(F32), grad[k], step, k)
        iterate[k] = value
        packed.append(value.astype(BF16))
    grads = times_gram(packed, high, low)
    for k in range(K):
        grad2[k] = grads[k]
    put_squares(grads, squares2)


def last_kernel(squares, iterate, grad, out):
    step = step_of(squares)
    for k in range(K):
        out[k] = proximal(iterate[k], grad[k], step, k)


def relay_kernel(rows, out):
    out[...] = jnp.broadcast_to(jnp.sum(rows[...], axis=0, keepdims=True), out.shape)


def call(kernel, shapes, *args):
    shapes = [jax.ShapeDtypeStruct(s, d) for s, d in shapes]
    return pl.pallas_call(
        kernel,
        out_shape=shapes,
        in_specs=[VMEM] * len(args),
        out_specs=[VMEM] * len(shapes),
        compiler_params=params(),
        name=kernel.__name__,
    )(*args)


def everywhere(rows):
    rows = lax.all_to_all(rows, ("xh", "y", "xl"), 0, 0, tiled=True)
    (rows,) = call(relay_kernel, [((32, BLK), F32)], rows)
    return lax.all_to_all(rows, ("z", "core"), 0, 0, tiled=True)


def swap(block, axis):
    return lax.ppermute(block, axis, [(0, 1), (1, 0)])


def swap_some(block, alike):
    route = [(0, 1), (3, 2)] if alike else [(1, 0), (2, 3)]
    return lax.ppermute(block, ("xh", "core"), route)


def along_z(block):
    depth, wide = SIZES[0], SIZES[1]
    route = []
    for z in range(depth):
        route.append((z * wide, (z + 1) % depth * wide))
        route.append((z * wide + 1, (z - 1) % depth * wide + 1))
    return lax.ppermute(block, ("z", "xh"), route)


def body(observed, pattern, omega_init):
    z, xh, core = (lax.axis_index(a) for a in VAR_AXES)
    samp = lax.axis_index("y") * 2 + lax.axis_index("xl")
    var = (z * 2 + xh) * 2 + core
    var_count = SIZES[0] * 4
    offset = (pattern // ROWB - var + var_count + 2) % var_count - 2
    near = jnp.where((offset == 1) == (core == 0), 1, 3)
    far = jnp.where((offset == 2) == (xh == 0), 2, 4)
    source = jnp.where(offset == 0, 0, jnp.where(abs(offset) == 1, near, far)).astype(jnp.int32)
    column = (pattern % ROWB).astype(jnp.int32)

    half = observed.shape[0] // 2
    partner = [swap(observed[:half], "core"), swap(observed[half:], "core")]
    edges = [sum(SIZES_OF_CHUNKS[:i]) for i in range(CHUNKS + 1)]
    across = [swap(observed[a:b], "xh") for a, b in zip(edges, edges[1:])]
    beyond = [along_z(a) for a in across]
    beside = [swap(jnp.where(core == xh, a, b), "core") for a, b in zip(across[:-1], beyond[:-1])]
    beside += [swap_some(across[-1], True), swap_some(beyond[-1], False)]
    strips = [observed, *partner, *across, *beside, *beyond]
    grams = on_strips(gram_kernel, (ROWB, GRAM_ROWS, BLK), [SMEM, SMEM], source, column, *strips)
    parts = lax.all_to_all(grams, SAMP_AXES, 0, 0, tiled=True)
    omega = lax.dynamic_index_in_dim(omega_init, samp, 0, keepdims=False)
    side = K * BLK
    blocks = (K, BLK, BLK)
    high, low, grad, squares = call(
        first_kernel,
        [((side, side), BF16), ((side, side), BF16), (blocks, F32), ((16, BLK), F32)],
        parts,
        omega,
    )
    iterate, grad, squares = call(
        second_kernel,
        [(blocks, F32), (blocks, F32), ((16, BLK), F32)],
        everywhere(squares),
        omega,
        grad,
        high,
        low,
    )
    (precision,) = call(last_kernel, [(blocks, F32)], everywhere(squares), iterate, grad)
    return precision[None]


def solution(mesh):
    fine = Mesh(mesh.devices.reshape(SIZES), AXES)
    return jax.shard_map(
        body,
        mesh=fine,
        in_specs=(P(SAMP_AXES, VAR_AXES), P(VAR_AXES, None), P(VAR_AXES, None, None, None)),
        out_specs=P(AXES, None, None, None),
        check_vma=False,
    )
```

```python
import jax
import jax.numpy as jnp
from jax import lax
from jax.experimental import pallas as pl
from jax.experimental.pallas import tpu as pltpu
from jax.sharding import Mesh, PartitionSpec as P

STEP_SCALE = 0.5
THRESHOLD = 0.25
EPSILON = 1e-06

AXES = ("z", "xh", "core", "y", "xl")
SIZES = (16, 2, 2, 4, 2)
VAR_AXES = ("z", "xh", "core")
SAMP_AXES = ("y", "xl")
SIZES_OF_CHUNKS = (192, 192, 128)
CHUNKS = len(SIZES_OF_CHUNKS)
ROWB = 8
K = 3
BLK = 128
SAMPLES = 4096
ENTRIES = 25165824
SAMP = 8
CROSS = ((0, 1), (0, 2), (1, 2))
HALF = BLK // 2
MIXED = 3 * BLK
FOLDED = 4 * BLK
DIAGS = FOLDED + HALF
GRAM_ROWS = DIAGS + 16

VMEM = pl.BlockSpec(memory_space=pltpu.VMEM)
SMEM = pl.BlockSpec(memory_space=pltpu.SMEM)
ANY = pl.BlockSpec(memory_space=pl.ANY)
F32 = jnp.float32
BF16 = jnp.bfloat16


def params():
    return pltpu.CompilerParams(vmem_limit_bytes=16 * 1024 * 1024)


def choose(inputs, held, source, column):
    def one(n, carry):
        r, k = n // (K - 1), n % (K - 1) + 1
        at = pl.ds(pl.multiple_of(column[r, k] * BLK, BLK), BLK)
        for slot in range(1, 5):

            @pl.when(source[r, k] == slot)
            def _():
                start = 0
                for strip in inputs[slot]:
                    rows = strip.shape[0]
                    held[n, pl.ds(start, rows), :] = strip[:, at]
                    start += rows

        return carry

    lax.fori_loop(0, ROWB * (K - 1), one, 0)


def dot(left, right, left_dim, right_dim):
    return lax.dot_general(
        left, right, (((left_dim,), (right_dim,)), ((), ())), preferred_element_type=F32
    )


def diagonal_mask():
    row = lax.broadcasted_iota(jnp.int32, (BLK, BLK), 0)
    col = lax.broadcasted_iota(jnp.int32, (BLK, BLK), 1)
    return row, col


def gram_kernel(source, column, *refs):
    *strips, out, held = refs
    inputs = [strips[:1], strips[1:2]]
    inputs += [strips[2 + CHUNKS * i : 2 + CHUNKS * (i + 1)] for i in range(3)]
    choose(inputs, held, source, column)
    row, col = diagonal_mask()
    line = lax.broadcasted_iota(jnp.int32, (16, BLK), 0)

    for r in range(ROWB):
        cols = [strips[0][:, r * BLK : (r + 1) * BLK], held[2 * r], held[2 * r + 1]]
        scaled = [
            dot(cols[i], jnp.concatenate(cols[i:], axis=1), 0, 0) * (1.0 / SAMPLES) for i in range(K)
        ]
        for p, (i, j) in enumerate(CROSS):
            at = (j - i) * BLK
            out[r, pl.ds(p * BLK, BLK), :] = scaled[i][:, at : at + BLK].astype(BF16)
        own = [block[:, :BLK] for block in scaled]
        top, bottom = own[2][:HALF], pltpu.roll(own[2][HALF:], HALF, 1)
        folded = jnp.where(row[:HALF] <= col[:HALF], top, bottom)
        out[r, pl.ds(FOLDED, HALF), :] = folded.astype(BF16)
        out[r, pl.ds(MIXED, BLK), :] = jnp.where(row <= col, own[0], own[1]).astype(BF16)
        lines = jnp.zeros((16, BLK), F32)
        for k in range(K):
            diag = jnp.sum(jnp.where(row == col, own[k], 0.0), axis=0, keepdims=True)
            high = diag.astype(BF16).astype(F32)
            lines = jnp.where(line == 2 * k, high, lines)
            lines = jnp.where(line == 2 * k + 1, diag - high, lines)
        out[r, pl.ds(DIAGS, 16), :] = lines.astype(BF16)


def on_strips(kernel, shape, specs, *args):
    arrays = args[len(specs) :]
    samples, columns = arrays[0].shape
    flops = 2 * ROWB * 6 * BLK * BLK * samples
    return pl.pallas_call(
        kernel,
        out_shape=jax.ShapeDtypeStruct(shape, BF16),
        in_specs=specs + [VMEM] * len(arrays),
        out_specs=VMEM,
        scratch_shapes=[pltpu.VMEM((ROWB * (K - 1), samples, BLK), BF16)],
        compiler_params=params(),
        cost_estimate=pl.CostEstimate(flops=flops, bytes_accessed=12 * samples * columns, transcendentals=0),
        name=kernel.__name__,
    )(*args)


def times_gram(packed, high, low):
    total = jnp.zeros((BLK, K * BLK), F32)
    for j in range(K):
        rows = slice(j * BLK, (j + 1) * BLK)
        total += jnp.dot(packed[j], high[rows, :], preferred_element_type=F32)
        total += jnp.dot(packed[j], low[rows, :], preferred_element_type=F32)
    return [total[:, k * BLK : (k + 1) * BLK] for k in range(K)]


def put_squares(grads, out):
    squares = sum(jnp.sum(g * g, axis=0, keepdims=True) for g in grads)
    out[...] = jnp.broadcast_to(squares, out.shape)


def first_kernel(parts, omega, high, low, grad, squares):
    def summed(start, count):
        return sum(parts[s, pl.ds(start, count), :].astype(F32) for s in range(SAMP))

    def put(i, j, block):
        at = (pl.ds(i * BLK, BLK), pl.ds(j * BLK, BLK))
        top = block.astype(BF16)
        high[at] = top
        low[at] = (block - top.astype(F32)).astype(BF16)

    row, col = diagonal_mask()
    lines = summed(DIAGS, 16)
    mixed = summed(MIXED, BLK)
    flipped = mixed.T
    folded = summed(FOLDED, HALF)
    unfolded = jnp.concatenate([folded, pltpu.roll(folded, HALF, 1)], axis=0)
    kept = ((row < HALF) & (row < col)) | ((col >= HALF) & (row > col))
    own = (
        jnp.where(row < col, mixed, flipped),
        jnp.where(row > col, mixed, flipped),
        jnp.where(kept, unfolded, unfolded.T),
    )
    for k in range(K):
        diag = lines[2 * k : 2 * k + 1, :] + lines[2 * k + 1 : 2 * k + 2, :]
        put(k, k, jnp.where(row == col, diag, own[k]))
    for p, (i, j) in enumerate(CROSS):
        block = summed(p * BLK, BLK)
        put(i, j, block)
        put(j, i, block.T)
    grads = times_gram(omega, high, low)
    for k in range(K):
        grad[k] = grads[k]
    put_squares(grads, squares)


def step_of(squares):
    mean_sq = jnp.sum(squares[...]) * (1.0 / ENTRIES)
    mean_sq = jnp.full((8, BLK), mean_sq, F32)
    return (STEP_SCALE / jnp.sqrt(mean_sq + EPSILON))[0:1, :]


def proximal(iterate, grad, step, k):
    stepped = iterate - step * grad
    shrunk = stepped - jnp.clip(stepped, -THRESHOLD, THRESHOLD)
    if k:
        return shrunk
    row, col = diagonal_mask()
    barrier = 0.5 * (stepped + jnp.sqrt(stepped * stepped + 4.0 * step))
    return jnp.where(row == col, barrier, shrunk)


def second_kernel(squares, omega, grad, high, low, iterate, grad2, squares2):
    step = step_of(squares)
    packed = []
    for k in range(K):
        value = proximal(omega[k].astype(F32), grad[k], step, k)
        iterate[k] = value
        packed.append(value.astype(BF16))
    grads = times_gram(packed, high, low)
    for k in range(K):
        grad2[k] = grads[k]
    put_squares(grads, squares2)


def last_kernel(squares, iterate, grad, out):
    step = step_of(squares)
    for k in range(K):
        out[k] = proximal(iterate[k], grad[k], step, k)


def relay_kernel(rows, out):
    out[...] = jnp.broadcast_to(jnp.sum(rows[...], axis=0, keepdims=True), out.shape)


def call(kernel, shapes, *args):
    shapes = [jax.ShapeDtypeStruct(s, d) for s, d in shapes]
    return pl.pallas_call(
        kernel,
        out_shape=shapes,
        in_specs=[VMEM] * len(args),
        out_specs=[VMEM] * len(shapes),
        compiler_params=params(),
        name=kernel.__name__,
    )(*args)


def everywhere(rows):
    rows = lax.all_to_all(rows, ("xh", "y", "xl"), 0, 0, tiled=True)
    (rows,) = call(relay_kernel, [((32, BLK), F32)], rows)
    return lax.all_to_all(rows, ("z", "core"), 0, 0, tiled=True)


def swap(block, axis):
    return lax.ppermute(block, axis, [(0, 1), (1, 0)])


def along_z(block):
    depth, wide = SIZES[0], SIZES[1]
    route = []
    for z in range(depth):
        route.append((z * wide, (z + 1) % depth * wide))
        route.append((z * wide + 1, (z - 1) % depth * wide + 1))
    return lax.ppermute(block, ("z", "xh"), route)


def straight(block):
    depth, wide = SIZES[0], SIZES[1]
    route = []
    for z in range(depth):
        route.append((z * wide + 1, (z + 1) % depth * wide))
        route.append((z * wide, (z - 1) % depth * wide + 1))
    return lax.ppermute(block, ("z", "xh"), route)


def body(observed, pattern, omega_init):
    z, xh, core = (lax.axis_index(a) for a in VAR_AXES)
    samp = lax.axis_index("y") * 2 + lax.axis_index("xl")
    var = (z * 2 + xh) * 2 + core
    var_count = SIZES[0] * 4
    offset = (pattern // ROWB - var + var_count + 2) % var_count - 2
    near = jnp.where((offset == 1) == (core == 0), 1, 3)
    far = jnp.where((offset == 2) == (xh == 0), 2, 4)
    source = jnp.where(offset == 0, 0, jnp.where(abs(offset) == 1, near, far)).astype(jnp.int32)
    column = (pattern % ROWB).astype(jnp.int32)

    edges = [sum(SIZES_OF_CHUNKS[:i]) for i in range(CHUNKS + 1)]
    pieces = [observed[a:b] for a, b in zip(edges, edges[1:])]
    across = [swap(a, "xh") for a in pieces]
    beyond = [along_z(a) for a in across[:-1]] + [straight(pieces[-1])]
    own, across[-1], beyond[-1] = lax.optimization_barrier((observed, across[-1], beyond[-1]))
    partner = swap(own, "core")
    beside = [swap(jnp.where(core == xh, a, b), "core") for a, b in zip(across, beyond)]
    strips = [observed, partner, *across, *beside, *beyond]
    grams = on_strips(gram_kernel, (ROWB, GRAM_ROWS, BLK), [SMEM, SMEM], source, column, *strips)
    parts = lax.all_to_all(grams, SAMP_AXES, 0, 0, tiled=True)
    omega = lax.dynamic_index_in_dim(omega_init, samp, 0, keepdims=False)
    side = K * BLK
    blocks = (K, BLK, BLK)
    high, low, grad, squares = call(
        first_kernel,
        [((side, side), BF16), ((side, side), BF16), (blocks, F32), ((16, BLK), F32)],
        parts,
        omega,
    )
    iterate, grad, squares = call(
        second_kernel,
        [(blocks, F32), (blocks, F32), ((16, BLK), F32)],
        everywhere(squares),
        omega,
        grad,
        high,
        low,
    )
    (precision,) = call(last_kernel, [(blocks, F32)], everywhere(squares), iterate, grad)
    return precision[None]


def solution(mesh):
    fine = Mesh(mesh.devices.reshape(SIZES), AXES)
    return jax.shard_map(
        body,
        mesh=fine,
        in_specs=(P(SAMP_AXES, VAR_AXES), P(VAR_AXES, None), P(VAR_AXES, None, None, None)),
        out_specs=P(AXES, None, None, None),
        check_vma=False,
    )
```

```python
import jax
import jax.numpy as jnp
from jax import lax
from jax.experimental import pallas as pl
from jax.experimental.pallas import tpu as pltpu
from jax.sharding import Mesh, PartitionSpec as P

STEP_SCALE = 0.5
THRESHOLD = 0.25
EPSILON = 1e-06

AXES = ("z", "xh", "core", "y", "xl")
SIZES = (16, 2, 2, 4, 2)
VAR_AXES = ("z", "xh", "core")
SAMP_AXES = ("y", "xl")
SIZES_OF_CHUNKS = (128, 192, 192)
CHUNKS = len(SIZES_OF_CHUNKS)
ROWB = 8
K = 3
BLK = 128
SAMPLES = 4096
ENTRIES = 25165824
SAMP = 8
CROSS = ((0, 1), (0, 2), (1, 2))
HALF = BLK // 2
MIXED = 3 * BLK
FOLDED = 4 * BLK
DIAGS = FOLDED + HALF
GRAM_ROWS = DIAGS + 16

VMEM = pl.BlockSpec(memory_space=pltpu.VMEM)
SMEM = pl.BlockSpec(memory_space=pltpu.SMEM)
ANY = pl.BlockSpec(memory_space=pl.ANY)
F32 = jnp.float32
BF16 = jnp.bfloat16


def params():
    return pltpu.CompilerParams(vmem_limit_bytes=16 * 1024 * 1024)


def choose(inputs, held, source, column):
    def one(n, carry):
        r, k = n // (K - 1), n % (K - 1) + 1
        at = pl.ds(pl.multiple_of(column[r, k] * BLK, BLK), BLK)
        for slot in range(1, 5):

            @pl.when(source[r, k] == slot)
            def _():
                start = 0
                for strip in inputs[slot]:
                    rows = strip.shape[0]
                    held[n, pl.ds(start, rows), :] = strip[:, at]
                    start += rows

        return carry

    lax.fori_loop(0, ROWB * (K - 1), one, 0)


def dot(left, right, left_dim, right_dim):
    return lax.dot_general(
        left, right, (((left_dim,), (right_dim,)), ((), ())), preferred_element_type=F32
    )


def diagonal_mask():
    row = lax.broadcasted_iota(jnp.int32, (BLK, BLK), 0)
    col = lax.broadcasted_iota(jnp.int32, (BLK, BLK), 1)
    return row, col


def gram_kernel(source, column, *refs):
    *strips, out, held = refs
    inputs = [strips[:1], strips[1:2]]
    inputs += [strips[a:b] for a, b in ((2, 5), (5, 7), (7, 10))]
    choose(inputs, held, source, column)
    row, col = diagonal_mask()
    line = lax.broadcasted_iota(jnp.int32, (16, BLK), 0)

    for r in range(ROWB):
        cols = [strips[0][:, r * BLK : (r + 1) * BLK], held[2 * r], held[2 * r + 1]]
        scaled = [
            dot(cols[i], jnp.concatenate(cols[i:], axis=1), 0, 0) * (1.0 / SAMPLES) for i in range(K)
        ]
        for p, (i, j) in enumerate(CROSS):
            at = (j - i) * BLK
            out[r, pl.ds(p * BLK, BLK), :] = scaled[i][:, at : at + BLK].astype(BF16)
        own = [block[:, :BLK] for block in scaled]
        top, bottom = own[2][:HALF], pltpu.roll(own[2][HALF:], HALF, 1)
        folded = jnp.where(row[:HALF] <= col[:HALF], top, bottom)
        out[r, pl.ds(FOLDED, HALF), :] = folded.astype(BF16)
        out[r, pl.ds(MIXED, BLK), :] = jnp.where(row <= col, own[0], own[1]).astype(BF16)
        lines = jnp.zeros((16, BLK), F32)
        for k in range(K):
            diag = jnp.sum(jnp.where(row == col, own[k], 0.0), axis=0, keepdims=True)
            high = diag.astype(BF16).astype(F32)
            lines = jnp.where(line == 2 * k, high, lines)
            lines = jnp.where(line == 2 * k + 1, diag - high, lines)
        out[r, pl.ds(DIAGS, 16), :] = lines.astype(BF16)


def on_strips(kernel, shape, specs, *args):
    arrays = args[len(specs) :]
    samples, columns = arrays[0].shape
    flops = 2 * ROWB * 6 * BLK * BLK * samples
    return pl.pallas_call(
        kernel,
        out_shape=jax.ShapeDtypeStruct(shape, BF16),
        in_specs=specs + [VMEM] * len(arrays),
        out_specs=VMEM,
        scratch_shapes=[pltpu.VMEM((ROWB * (K - 1), samples, BLK), BF16)],
        compiler_params=params(),
        cost_estimate=pl.CostEstimate(flops=flops, bytes_accessed=12 * samples * columns, transcendentals=0),
        name=kernel.__name__,
    )(*args)


def times_gram(packed, high, low):
    total = jnp.zeros((BLK, K * BLK), F32)
    for j in range(K):
        rows = slice(j * BLK, (j + 1) * BLK)
        total += jnp.dot(packed[j], high[rows, :], preferred_element_type=F32)
        total += jnp.dot(packed[j], low[rows, :], preferred_element_type=F32)
    return [total[:, k * BLK : (k + 1) * BLK] for k in range(K)]


def put_squares(grads, out):
    squares = sum(jnp.sum(g * g, axis=0, keepdims=True) for g in grads)
    out[...] = jnp.broadcast_to(squares, out.shape)


def first_kernel(parts, omega, high, low, grad, squares):
    def summed(start, count):
        return sum(parts[s, pl.ds(start, count), :].astype(F32) for s in range(SAMP))

    def put(i, j, block):
        at = (pl.ds(i * BLK, BLK), pl.ds(j * BLK, BLK))
        top = block.astype(BF16)
        high[at] = top
        low[at] = (block - top.astype(F32)).astype(BF16)

    row, col = diagonal_mask()
    lines = summed(DIAGS, 16)
    mixed = summed(MIXED, BLK)
    flipped = mixed.T
    folded = summed(FOLDED, HALF)
    unfolded = jnp.concatenate([folded, pltpu.roll(folded, HALF, 1)], axis=0)
    kept = ((row < HALF) & (row < col)) | ((col >= HALF) & (row > col))
    own = (
        jnp.where(row < col, mixed, flipped),
        jnp.where(row > col, mixed, flipped),
        jnp.where(kept, unfolded, unfolded.T),
    )
    for k in range(K):
        diag = lines[2 * k : 2 * k + 1, :] + lines[2 * k + 1 : 2 * k + 2, :]
        put(k, k, jnp.where(row == col, diag, own[k]))
    for p, (i, j) in enumerate(CROSS):
        block = summed(p * BLK, BLK)
        put(i, j, block)
        put(j, i, block.T)
    grads = times_gram(omega, high, low)
    for k in range(K):
        grad[k] = grads[k]
    put_squares(grads, squares)


def step_of(squares):
    mean_sq = jnp.sum(squares[...]) * (1.0 / ENTRIES)
    mean_sq = jnp.full((8, BLK), mean_sq, F32)
    return (STEP_SCALE / jnp.sqrt(mean_sq + EPSILON))[0:1, :]


def proximal(iterate, grad, step, k):
    stepped = iterate - step * grad
    shrunk = stepped - jnp.clip(stepped, -THRESHOLD, THRESHOLD)
    if k:
        return shrunk
    row, col = diagonal_mask()
    barrier = 0.5 * (stepped + jnp.sqrt(stepped * stepped + 4.0 * step))
    return jnp.where(row == col, barrier, shrunk)


def second_kernel(squares, omega, grad, high, low, iterate, grad2, squares2):
    step = step_of(squares)
    packed = []
    for k in range(K):
        value = proximal(omega[k].astype(F32), grad[k], step, k)
        iterate[k] = value
        packed.append(value.astype(BF16))
    grads = times_gram(packed, high, low)
    for k in range(K):
        grad2[k] = grads[k]
    put_squares(grads, squares2)


def last_kernel(squares, iterate, grad, out):
    step = step_of(squares)
    for k in range(K):
        out[k] = proximal(iterate[k], grad[k], step, k)


def relay_kernel(rows, out):
    out[...] = jnp.broadcast_to(jnp.sum(rows[...], axis=0, keepdims=True), out.shape)


def call(kernel, shapes, *args):
    shapes = [jax.ShapeDtypeStruct(s, d) for s, d in shapes]
    return pl.pallas_call(
        kernel,
        out_shape=shapes,
        in_specs=[VMEM] * len(args),
        out_specs=[VMEM] * len(shapes),
        compiler_params=params(),
        name=kernel.__name__,
    )(*args)


def everywhere(rows):
    rows = lax.all_to_all(rows, ("xh", "y", "xl"), 0, 0, tiled=True)
    (rows,) = call(relay_kernel, [((32, BLK), F32)], rows)
    return lax.all_to_all(rows, ("z", "core"), 0, 0, tiled=True)


def swap(block, axis):
    return lax.ppermute(block, axis, [(0, 1), (1, 0)])


def along_z(block):
    depth, wide = SIZES[0], SIZES[1]
    route = []
    for z in range(depth):
        route.append((z * wide, (z + 1) % depth * wide))
        route.append((z * wide + 1, (z - 1) % depth * wide + 1))
    return lax.ppermute(block, ("z", "xh"), route)


def straight(block):
    depth, wide = SIZES[0], SIZES[1]
    route = []
    for z in range(depth):
        route.append((z * wide + 1, (z + 1) % depth * wide))
        route.append((z * wide, (z - 1) % depth * wide + 1))
    return lax.ppermute(block, ("z", "xh"), route)


def body(observed, pattern, omega_init):
    z, xh, core = (lax.axis_index(a) for a in VAR_AXES)
    samp = lax.axis_index("y") * 2 + lax.axis_index("xl")
    var = (z * 2 + xh) * 2 + core
    var_count = SIZES[0] * 4
    offset = (pattern // ROWB - var + var_count + 2) % var_count - 2
    near = jnp.where((offset == 1) == (core == 0), 1, 3)
    far = jnp.where((offset == 2) == (xh == 0), 2, 4)
    source = jnp.where(offset == 0, 0, jnp.where(abs(offset) == 1, near, far)).astype(jnp.int32)
    column = (pattern % ROWB).astype(jnp.int32)

    edges = [sum(SIZES_OF_CHUNKS[:i]) for i in range(CHUNKS + 1)]
    pieces = [observed[a:b] for a, b in zip(edges, edges[1:])]
    partner = swap(observed, "core")
    across = [swap(a, "xh") for a in pieces]
    beyond = [straight(pieces[0])] + [along_z(a) for a in across[1:]]
    here, there = jnp.concatenate(across[:2]), jnp.concatenate(beyond[:2])
    beside = [
        swap(jnp.where(core == xh, here, there), "core"),
        swap(jnp.where(core == xh, across[2], beyond[2]), "core"),
    ]
    strips = [observed, partner, *across, *beside, *beyond]
    grams = on_strips(gram_kernel, (ROWB, GRAM_ROWS, BLK), [SMEM, SMEM], source, column, *strips)
    parts = lax.all_to_all(grams, SAMP_AXES, 0, 0, tiled=True)
    omega = lax.dynamic_index_in_dim(omega_init, samp, 0, keepdims=False)
    side = K * BLK
    blocks = (K, BLK, BLK)
    high, low, grad, squares = call(
        first_kernel,
        [((side, side), BF16), ((side, side), BF16), (blocks, F32), ((16, BLK), F32)],
        parts,
        omega,
    )
    iterate, grad, squares = call(
        second_kernel,
        [(blocks, F32), (blocks, F32), ((16, BLK), F32)],
        everywhere(squares),
        omega,
        grad,
        high,
        low,
    )
    (precision,) = call(last_kernel, [(blocks, F32)], everywhere(squares), iterate, grad)
    return precision[None]


def solution(mesh):
    fine = Mesh(mesh.devices.reshape(SIZES), AXES)
    return jax.shard_map(
        body,
        mesh=fine,
        in_specs=(P(SAMP_AXES, VAR_AXES), P(VAR_AXES, None), P(VAR_AXES, None, None, None)),
        out_specs=P(AXES, None, None, None),
        check_vma=False,
    )
```

```python
import jax
import jax.numpy as jnp
from jax import lax
from jax.experimental import pallas as pl
from jax.experimental.pallas import tpu as pltpu
from jax.sharding import Mesh, PartitionSpec as P

STEP_SCALE = 0.5
THRESHOLD = 0.25
EPSILON = 1e-06

AXES = ("z", "xh", "core", "y", "xl")
SIZES = (16, 2, 2, 4, 2)
VAR_AXES = ("z", "xh", "core")
SAMP_AXES = ("y", "xl")
SIZES_OF_CHUNKS = (128, 192, 192)
CHUNKS = len(SIZES_OF_CHUNKS)
ROWB = 8
K = 3
BLK = 128
SAMPLES = 4096
ENTRIES = 25165824
SAMP = 8
CROSS = ((0, 1), (0, 2), (1, 2))
HALF = BLK // 2
MIXED = 3 * BLK
FOLDED = 4 * BLK
DIAGS = FOLDED + HALF
GRAM_ROWS = DIAGS + 16

VMEM = pl.BlockSpec(memory_space=pltpu.VMEM)
SMEM = pl.BlockSpec(memory_space=pltpu.SMEM)
ANY = pl.BlockSpec(memory_space=pl.ANY)
F32 = jnp.float32
BF16 = jnp.bfloat16


def params():
    return pltpu.CompilerParams(vmem_limit_bytes=16 * 1024 * 1024)


def choose(inputs, held, source, column):
    def one(n, carry):
        r, k = n // (K - 1), n % (K - 1) + 1
        at = pl.ds(pl.multiple_of(column[r, k] * BLK, BLK), BLK)
        for slot in range(1, 5):

            @pl.when(source[r, k] == slot)
            def _():
                start = 0
                for strip in inputs[slot]:
                    rows = strip.shape[0]
                    held[n, pl.ds(start, rows), :] = strip[:, at]
                    start += rows

        return carry

    lax.fori_loop(0, ROWB * (K - 1), one, 0)


def dot(left, right, left_dim, right_dim):
    return lax.dot_general(
        left, right, (((left_dim,), (right_dim,)), ((), ())), preferred_element_type=F32
    )


def diagonal_mask():
    row = lax.broadcasted_iota(jnp.int32, (BLK, BLK), 0)
    col = lax.broadcasted_iota(jnp.int32, (BLK, BLK), 1)
    return row, col


def gram_kernel(source, column, *refs):
    *strips, out, held = refs
    inputs = [strips[:1], strips[1:2]]
    inputs += [strips[a:b] for a, b in ((2, 5), (5, 7), (7, 10))]
    choose(inputs, held, source, column)
    row, col = diagonal_mask()
    line = lax.broadcasted_iota(jnp.int32, (16, BLK), 0)

    for r in range(ROWB):
        cols = [strips[0][:, r * BLK : (r + 1) * BLK], held[2 * r], held[2 * r + 1]]
        scaled = [
            dot(cols[i], jnp.concatenate(cols[i:], axis=1), 0, 0) * (1.0 / SAMPLES) for i in range(K)
        ]
        for p, (i, j) in enumerate(CROSS):
            at = (j - i) * BLK
            out[r, pl.ds(p * BLK, BLK), :] = scaled[i][:, at : at + BLK].astype(BF16)
        own = [block[:, :BLK] for block in scaled]
        top, bottom = own[2][:HALF], pltpu.roll(own[2][HALF:], HALF, 1)
        folded = jnp.where(row[:HALF] <= col[:HALF], top, bottom)
        out[r, pl.ds(FOLDED, HALF), :] = folded.astype(BF16)
        out[r, pl.ds(MIXED, BLK), :] = jnp.where(row <= col, own[0], own[1]).astype(BF16)
        lines = jnp.zeros((16, BLK), F32)
        for k in range(K):
            diag = jnp.sum(jnp.where(row == col, own[k], 0.0), axis=0, keepdims=True)
            high = diag.astype(BF16).astype(F32)
            lines = jnp.where(line == 2 * k, high, lines)
            lines = jnp.where(line == 2 * k + 1, diag - high, lines)
        out[r, pl.ds(DIAGS, 16), :] = lines.astype(BF16)


def on_strips(kernel, shape, specs, *args):
    arrays = args[len(specs) :]
    samples, columns = arrays[0].shape
    flops = 2 * ROWB * 6 * BLK * BLK * samples
    return pl.pallas_call(
        kernel,
        out_shape=jax.ShapeDtypeStruct(shape, BF16),
        in_specs=specs + [VMEM] * len(arrays),
        out_specs=VMEM,
        scratch_shapes=[pltpu.VMEM((ROWB * (K - 1), samples, BLK), BF16)],
        compiler_params=params(),
        cost_estimate=pl.CostEstimate(flops=flops, bytes_accessed=12 * samples * columns, transcendentals=0),
        name=kernel.__name__,
    )(*args)


def times_gram(packed, high, low):
    total = jnp.zeros((BLK, K * BLK), F32)
    for j in range(K):
        rows = slice(j * BLK, (j + 1) * BLK)
        total += jnp.dot(packed[j], high[rows, :], preferred_element_type=F32)
        total += jnp.dot(packed[j], low[rows, :], preferred_element_type=F32)
    return [total[:, k * BLK : (k + 1) * BLK] for k in range(K)]


def put_squares(grads, out):
    squares = sum(jnp.sum(g * g, axis=0, keepdims=True) for g in grads)
    out[...] = jnp.broadcast_to(squares, out.shape)


def first_kernel(parts, omega, high, low, grad, squares):
    def summed(start, count):
        return sum(parts[s, pl.ds(start, count), :].astype(F32) for s in range(SAMP))

    def put(i, j, block):
        at = (pl.ds(i * BLK, BLK), pl.ds(j * BLK, BLK))
        top = block.astype(BF16)
        high[at] = top
        low[at] = (block - top.astype(F32)).astype(BF16)

    row, col = diagonal_mask()
    lines = summed(DIAGS, 16)
    mixed = summed(MIXED, BLK)
    flipped = mixed.T
    folded = summed(FOLDED, HALF)
    unfolded = jnp.concatenate([folded, pltpu.roll(folded, HALF, 1)], axis=0)
    kept = ((row < HALF) & (row < col)) | ((col >= HALF) & (row > col))
    own = (
        jnp.where(row < col, mixed, flipped),
        jnp.where(row > col, mixed, flipped),
        jnp.where(kept, unfolded, unfolded.T),
    )
    for k in range(K):
        diag = lines[2 * k : 2 * k + 1, :] + lines[2 * k + 1 : 2 * k + 2, :]
        put(k, k, jnp.where(row == col, diag, own[k]))
    for p, (i, j) in enumerate(CROSS):
        block = summed(p * BLK, BLK)
        put(i, j, block)
        put(j, i, block.T)
    grads = times_gram(omega, high, low)
    for k in range(K):
        grad[k] = grads[k]
    put_squares(grads, squares)


def step_of(squares):
    mean_sq = jnp.sum(squares[...]) * (1.0 / ENTRIES)
    mean_sq = jnp.full((8, BLK), mean_sq, F32)
    return (STEP_SCALE / jnp.sqrt(mean_sq + EPSILON))[0:1, :]


def proximal(iterate, grad, step, k):
    stepped = iterate - step * grad
    shrunk = stepped - jnp.clip(stepped, -THRESHOLD, THRESHOLD)
    if k:
        return shrunk
    row, col = diagonal_mask()
    barrier = 0.5 * (stepped + jnp.sqrt(stepped * stepped + 4.0 * step))
    return jnp.where(row == col, barrier, shrunk)


def second_kernel(squares, omega, grad, high, low, iterate, grad2, squares2):
    step = step_of(squares)
    packed = []
    for k in range(K):
        value = proximal(omega[k].astype(F32), grad[k], step, k)
        iterate[k] = value
        packed.append(value.astype(BF16))
    grads = times_gram(packed, high, low)
    for k in range(K):
        grad2[k] = grads[k]
    put_squares(grads, squares2)


def last_kernel(squares, iterate, grad, out):
    step = step_of(squares)
    for k in range(K):
        out[k] = proximal(iterate[k], grad[k], step, k)


def relay_kernel(rows, out):
    out[...] = jnp.broadcast_to(jnp.sum(rows[...], axis=0, keepdims=True), out.shape)


def call(kernel, shapes, *args):
    shapes = [jax.ShapeDtypeStruct(s, d) for s, d in shapes]
    return pl.pallas_call(
        kernel,
        out_shape=shapes,
        in_specs=[VMEM] * len(args),
        out_specs=[VMEM] * len(shapes),
        compiler_params=params(),
        name=kernel.__name__,
    )(*args)


def everywhere(rows):
    rows = lax.all_to_all(rows, ("xh", "y", "xl"), 0, 0, tiled=True)
    (rows,) = call(relay_kernel, [((32, BLK), F32)], rows)
    return lax.all_to_all(rows, ("z", "core"), 0, 0, tiled=True)


def swap(block, axis):
    return lax.ppermute(block, axis, [(0, 1), (1, 0)])


def along_z(block):
    depth, wide = SIZES[0], SIZES[1]
    route = []
    for z in range(depth):
        route.append((z * wide, (z + 1) % depth * wide))
        route.append((z * wide + 1, (z - 1) % depth * wide + 1))
    return lax.ppermute(block, ("z", "xh"), route)


def straight(block):
    depth, wide = SIZES[0], SIZES[1]
    route = []
    for z in range(depth):
        route.append((z * wide + 1, (z + 1) % depth * wide))
        route.append((z * wide, (z - 1) % depth * wide + 1))
    return lax.ppermute(block, ("z", "xh"), route)


def body(observed, pattern, omega_init):
    z, xh, core = (lax.axis_index(a) for a in VAR_AXES)
    samp = lax.axis_index("y") * 2 + lax.axis_index("xl")
    var = (z * 2 + xh) * 2 + core
    var_count = SIZES[0] * 4
    offset = (pattern // ROWB - var + var_count + 2) % var_count - 2
    near = jnp.where((offset == 1) == (core == 0), 1, 3)
    far = jnp.where((offset == 2) == (xh == 0), 2, 4)
    source = jnp.where(offset == 0, 0, jnp.where(abs(offset) == 1, near, far)).astype(jnp.int32)
    column = (pattern % ROWB).astype(jnp.int32)

    edges = [sum(SIZES_OF_CHUNKS[:i]) for i in range(CHUNKS + 1)]
    pieces = [observed[a:b] for a, b in zip(edges, edges[1:])]
    partner = swap(observed, "core")
    across = [swap(a, "xh") for a in pieces]
    beyond = [straight(pieces[0])] + [along_z(a) for a in across[1:]]
    partner, across[0] = lax.optimization_barrier((partner, across[0]))
    here, there = jnp.concatenate(across[:2]), jnp.concatenate(beyond[:2])
    beside = [
        swap(jnp.where(core == xh, here, there), "core"),
        swap(jnp.where(core == xh, across[2], beyond[2]), "core"),
    ]
    strips = [observed, partner, *across, *beside, *beyond]
    grams = on_strips(gram_kernel, (ROWB, GRAM_ROWS, BLK), [SMEM, SMEM], source, column, *strips)
    parts = lax.all_to_all(grams, SAMP_AXES, 0, 0, tiled=True)
    omega = lax.dynamic_index_in_dim(omega_init, samp, 0, keepdims=False)
    side = K * BLK
    blocks = (K, BLK, BLK)
    high, low, grad, squares = call(
        first_kernel,
        [((side, side), BF16), ((side, side), BF16), (blocks, F32), ((16, BLK), F32)],
        parts,
        omega,
    )
    iterate, grad, squares = call(
        second_kernel,
        [(blocks, F32), (blocks, F32), ((16, BLK), F32)],
        everywhere(squares),
        omega,
        grad,
        high,
        low,
    )
    (precision,) = call(last_kernel, [(blocks, F32)], everywhere(squares), iterate, grad)
    return precision[None]


def solution(mesh):
    fine = Mesh(mesh.devices.reshape(SIZES), AXES)
    return jax.shard_map(
        body,
        mesh=fine,
        in_specs=(P(SAMP_AXES, VAR_AXES), P(VAR_AXES, None), P(VAR_AXES, None, None, None)),
        out_specs=P(AXES, None, None, None),
        check_vma=False,
    )
```

```python
import jax
import jax.numpy as jnp
from jax import lax
from jax.experimental import pallas as pl
from jax.experimental.pallas import tpu as pltpu
from jax.sharding import Mesh, PartitionSpec as P

STEP_SCALE = 0.5
THRESHOLD = 0.25
EPSILON = 1e-06

AXES = ("z", "xh", "core", "y", "xl")
SIZES = (16, 2, 2, 4, 2)
VAR_AXES = ("z", "xh", "core")
SAMP_AXES = ("y", "xl")
SIZES_OF_CHUNKS = (128, 208, 176)
CHUNKS = len(SIZES_OF_CHUNKS)
ROWB = 8
K = 3
BLK = 128
SAMPLES = 4096
ENTRIES = 25165824
SAMP = 8
CROSS = ((0, 1), (0, 2), (1, 2))
HALF = BLK // 2
MIXED = 3 * BLK
FOLDED = 4 * BLK
DIAGS = FOLDED + HALF
GRAM_ROWS = DIAGS + 16

VMEM = pl.BlockSpec(memory_space=pltpu.VMEM)
SMEM = pl.BlockSpec(memory_space=pltpu.SMEM)
ANY = pl.BlockSpec(memory_space=pl.ANY)
F32 = jnp.float32
BF16 = jnp.bfloat16


def params():
    return pltpu.CompilerParams(vmem_limit_bytes=16 * 1024 * 1024)


def choose(inputs, held, source, column):
    def one(n, carry):
        r, k = n // (K - 1), n % (K - 1) + 1
        at = pl.ds(pl.multiple_of(column[r, k] * BLK, BLK), BLK)
        for slot in range(1, 5):

            @pl.when(source[r, k] == slot)
            def _():
                start = 0
                for strip in inputs[slot]:
                    rows = strip.shape[0]
                    held[n, pl.ds(start, rows), :] = strip[:, at]
                    start += rows

        return carry

    lax.fori_loop(0, ROWB * (K - 1), one, 0, unroll=True)


def dot(left, right, left_dim, right_dim):
    return lax.dot_general(
        left, right, (((left_dim,), (right_dim,)), ((), ())), preferred_element_type=F32
    )


def diagonal_mask():
    row = lax.broadcasted_iota(jnp.int32, (BLK, BLK), 0)
    col = lax.broadcasted_iota(jnp.int32, (BLK, BLK), 1)
    return row, col


def gram_kernel(source, column, *refs):
    *strips, out, held = refs
    inputs = [strips[:1], strips[1:2]]
    inputs += [strips[a:b] for a, b in ((2, 5), (5, 7), (7, 10))]
    choose(inputs, held, source, column)
    row, col = diagonal_mask()
    line = lax.broadcasted_iota(jnp.int32, (16, BLK), 0)

    for r in range(ROWB):
        cols = [strips[0][:, r * BLK : (r + 1) * BLK], held[2 * r], held[2 * r + 1]]
        scaled = [
            dot(cols[i], jnp.concatenate(cols[i:], axis=1), 0, 0) * (1.0 / SAMPLES) for i in range(K)
        ]
        for p, (i, j) in enumerate(CROSS):
            at = (j - i) * BLK
            out[r, pl.ds(p * BLK, BLK), :] = scaled[i][:, at : at + BLK].astype(BF16)
        own = [block[:, :BLK] for block in scaled]
        top, bottom = own[2][:HALF], pltpu.roll(own[2][HALF:], HALF, 1)
        folded = jnp.where(row[:HALF] <= col[:HALF], top, bottom)
        out[r, pl.ds(FOLDED, HALF), :] = folded.astype(BF16)
        out[r, pl.ds(MIXED, BLK), :] = jnp.where(row <= col, own[0], own[1]).astype(BF16)
        lines = jnp.zeros((16, BLK), F32)
        for k in range(K):
            diag = jnp.sum(jnp.where(row == col, own[k], 0.0), axis=0, keepdims=True)
            high = diag.astype(BF16).astype(F32)
            lines = jnp.where(line == 2 * k, high, lines)
            lines = jnp.where(line == 2 * k + 1, diag - high, lines)
        out[r, pl.ds(DIAGS, 16), :] = lines.astype(BF16)


def on_strips(kernel, shape, specs, *args):
    arrays = args[len(specs) :]
    samples, columns = arrays[0].shape
    flops = 2 * ROWB * 6 * BLK * BLK * samples
    return pl.pallas_call(
        kernel,
        out_shape=jax.ShapeDtypeStruct(shape, BF16),
        in_specs=specs + [VMEM] * len(arrays),
        out_specs=VMEM,
        scratch_shapes=[pltpu.VMEM((ROWB * (K - 1), samples, BLK), BF16)],
        compiler_params=params(),
        cost_estimate=pl.CostEstimate(flops=flops, bytes_accessed=12 * samples * columns, transcendentals=0),
        name=kernel.__name__,
    )(*args)


def times_gram(packed, high, low):
    total = jnp.zeros((BLK, K * BLK), F32)
    for j in range(K):
        rows = slice(j * BLK, (j + 1) * BLK)
        total += jnp.dot(packed[j], high[rows, :], preferred_element_type=F32)
        total += jnp.dot(packed[j], low[rows, :], preferred_element_type=F32)
    return [total[:, k * BLK : (k + 1) * BLK] for k in range(K)]


def put_squares(grads, out):
    squares = sum(jnp.sum(g * g, axis=0, keepdims=True) for g in grads)
    out[...] = jnp.broadcast_to(squares, out.shape)


def first_kernel(parts, omega, high, low, grad, squares):
    def summed(start, count):
        return sum(parts[s, pl.ds(start, count), :].astype(F32) for s in range(SAMP))

    def put(i, j, block):
        at = (pl.ds(i * BLK, BLK), pl.ds(j * BLK, BLK))
        top = block.astype(BF16)
        high[at] = top
        low[at] = (block - top.astype(F32)).astype(BF16)

    row, col = diagonal_mask()
    lines = summed(DIAGS, 16)
    mixed = summed(MIXED, BLK)
    flipped = mixed.T
    folded = summed(FOLDED, HALF)
    unfolded = jnp.concatenate([folded, pltpu.roll(folded, HALF, 1)], axis=0)
    kept = ((row < HALF) & (row < col)) | ((col >= HALF) & (row > col))
    own = (
        jnp.where(row < col, mixed, flipped),
        jnp.where(row > col, mixed, flipped),
        jnp.where(kept, unfolded, unfolded.T),
    )
    for k in range(K):
        diag = lines[2 * k : 2 * k + 1, :] + lines[2 * k + 1 : 2 * k + 2, :]
        put(k, k, jnp.where(row == col, diag, own[k]))
    for p, (i, j) in enumerate(CROSS):
        block = summed(p * BLK, BLK)
        put(i, j, block)
        put(j, i, block.T)
    grads = times_gram(omega, high, low)
    for k in range(K):
        grad[k] = grads[k]
    put_squares(grads, squares)


def step_of(squares):
    mean_sq = jnp.sum(squares[...]) * (1.0 / ENTRIES)
    mean_sq = jnp.full((8, BLK), mean_sq, F32)
    return (STEP_SCALE / jnp.sqrt(mean_sq + EPSILON))[0:1, :]


def proximal(iterate, grad, step, k):
    stepped = iterate - step * grad
    shrunk = stepped - jnp.clip(stepped, -THRESHOLD, THRESHOLD)
    if k:
        return shrunk
    row, col = diagonal_mask()
    barrier = 0.5 * (stepped + jnp.sqrt(stepped * stepped + 4.0 * step))
    return jnp.where(row == col, barrier, shrunk)


def second_kernel(squares, omega, grad, high, low, iterate, grad2, squares2):
    step = step_of(squares)
    packed = []
    for k in range(K):
        value = proximal(omega[k].astype(F32), grad[k], step, k)
        iterate[k] = value
        packed.append(value.astype(BF16))
    grads = times_gram(packed, high, low)
    for k in range(K):
        grad2[k] = grads[k]
    put_squares(grads, squares2)


def last_kernel(squares, iterate, grad, out):
    step = step_of(squares)
    for k in range(K):
        out[k] = proximal(iterate[k], grad[k], step, k)


def relay_kernel(rows, out):
    out[...] = jnp.broadcast_to(jnp.sum(rows[...], axis=0, keepdims=True), out.shape)


def call(kernel, shapes, *args):
    shapes = [jax.ShapeDtypeStruct(s, d) for s, d in shapes]
    return pl.pallas_call(
        kernel,
        out_shape=shapes,
        in_specs=[VMEM] * len(args),
        out_specs=[VMEM] * len(shapes),
        compiler_params=params(),
        name=kernel.__name__,
    )(*args)


def everywhere(rows):
    rows = lax.all_to_all(rows, ("xh", "y", "xl"), 0, 0, tiled=True)
    (rows,) = call(relay_kernel, [((32, BLK), F32)], rows)
    return lax.all_to_all(rows, ("z", "core"), 0, 0, tiled=True)


def swap(block, axis):
    return lax.ppermute(block, axis, [(0, 1), (1, 0)])


def along_z(block):
    depth, wide = SIZES[0], SIZES[1]
    route = []
    for z in range(depth):
        route.append((z * wide, (z + 1) % depth * wide))
        route.append((z * wide + 1, (z - 1) % depth * wide + 1))
    return lax.ppermute(block, ("z", "xh"), route)


def straight(block):
    depth, wide = SIZES[0], SIZES[1]
    route = []
    for z in range(depth):
        route.append((z * wide + 1, (z + 1) % depth * wide))
        route.append((z * wide, (z - 1) % depth * wide + 1))
    return lax.ppermute(block, ("z", "xh"), route)


def body(observed, pattern, omega_init):
    z, xh, core = (lax.axis_index(a) for a in VAR_AXES)
    samp = lax.axis_index("y") * 2 + lax.axis_index("xl")
    var = (z * 2 + xh) * 2 + core
    var_count = SIZES[0] * 4
    offset = (pattern // ROWB - var + var_count + 2) % var_count - 2
    near = jnp.where((offset == 1) == (core == 0), 1, 3)
    far = jnp.where((offset == 2) == (xh == 0), 2, 4)
    source = jnp.where(offset == 0, 0, jnp.where(abs(offset) == 1, near, far)).astype(jnp.int32)
    column = (pattern % ROWB).astype(jnp.int32)

    edges = [sum(SIZES_OF_CHUNKS[:i]) for i in range(CHUNKS + 1)]
    pieces = [observed[a:b] for a, b in zip(edges, edges[1:])]
    partner = swap(observed, "core")
    across = [swap(a, "xh") for a in pieces]
    beyond = [straight(pieces[0])] + [along_z(a) for a in across[1:]]
    partner, across[0] = lax.optimization_barrier((partner, across[0]))
    here, there = jnp.concatenate(across[:2]), jnp.concatenate(beyond[:2])
    beside = [
        swap(jnp.where(core == xh, here, there), "core"),
        swap(jnp.where(core == xh, across[2], beyond[2]), "core"),
    ]
    strips = [observed, partner, *across, *beside, *beyond]
    grams = on_strips(gram_kernel, (ROWB, GRAM_ROWS, BLK), [SMEM, SMEM], source, column, *strips)
    parts = lax.all_to_all(grams, SAMP_AXES, 0, 0, tiled=True)
    omega = lax.dynamic_index_in_dim(omega_init, samp, 0, keepdims=False)
    side = K * BLK
    blocks = (K, BLK, BLK)
    high, low, grad, squares = call(
        first_kernel,
        [((side, side), BF16), ((side, side), BF16), (blocks, F32), ((16, BLK), F32)],
        parts,
        omega,
    )
    iterate, grad, squares = call(
        second_kernel,
        [(blocks, F32), (blocks, F32), ((16, BLK), F32)],
        everywhere(squares),
        omega,
        grad,
        high,
        low,
    )
    (precision,) = call(last_kernel, [(blocks, F32)], everywhere(squares), iterate, grad)
    return precision[None]


def solution(mesh):
    fine = Mesh(mesh.devices.reshape(SIZES), AXES)
    return jax.shard_map(
        body,
        mesh=fine,
        in_specs=(P(SAMP_AXES, VAR_AXES), P(VAR_AXES, None), P(VAR_AXES, None, None, None)),
        out_specs=P(AXES, None, None, None),
        check_vma=False,
    )
```

```python
import jax
import jax.numpy as jnp
from jax import lax
from jax.experimental import pallas as pl
from jax.experimental.pallas import tpu as pltpu
from jax.sharding import Mesh, PartitionSpec as P

STEP_SCALE = 0.5
THRESHOLD = 0.25
EPSILON = 1e-06

AXES = ("z", "xh", "core", "y", "xl")
SIZES = (16, 2, 2, 4, 2)
VAR_AXES = ("z", "xh", "core")
SAMP_AXES = ("y", "xl")
SIZES_OF_CHUNKS = (128, 192, 192)
CHUNKS = len(SIZES_OF_CHUNKS)
ROWB = 8
K = 3
BLK = 128
SAMPLES = 4096
ENTRIES = 25165824
SAMP = 8
CROSS = ((0, 1), (0, 2), (1, 2))
HALF = BLK // 2
MIXED = 3 * BLK
FOLDED = 4 * BLK
DIAGS = FOLDED + HALF
GRAM_ROWS = DIAGS + 16

VMEM = pl.BlockSpec(memory_space=pltpu.VMEM)
SMEM = pl.BlockSpec(memory_space=pltpu.SMEM)
ANY = pl.BlockSpec(memory_space=pl.ANY)
F32 = jnp.float32
BF16 = jnp.bfloat16


def params():
    return pltpu.CompilerParams(vmem_limit_bytes=16 * 1024 * 1024)


def choose(inputs, held, source, column):
    def one(n, carry):
        r, k = n // (K - 1), n % (K - 1) + 1
        at = pl.ds(pl.multiple_of(column[r, k] * BLK, BLK), BLK)
        for slot in range(1, 5):

            @pl.when(source[r, k] == slot)
            def _():
                start = 0
                for strip in inputs[slot]:
                    rows = strip.shape[0]
                    held[n, pl.ds(start, rows), :] = strip[:, at]
                    start += rows

        return carry

    lax.fori_loop(0, ROWB * (K - 1), one, 0, unroll=True)


def dot(left, right, left_dim, right_dim):
    return lax.dot_general(
        left, right, (((left_dim,), (right_dim,)), ((), ())), preferred_element_type=F32
    )


def diagonal_mask():
    row = lax.broadcasted_iota(jnp.int32, (BLK, BLK), 0)
    col = lax.broadcasted_iota(jnp.int32, (BLK, BLK), 1)
    return row, col


def gram_kernel(source, column, *refs):
    *strips, out, held = refs
    inputs = [strips[:1], strips[1:2]]
    inputs += [strips[a:b] for a, b in ((2, 5), (5, 7), (7, 10))]
    choose(inputs, held, source, column)
    row, col = diagonal_mask()
    line = lax.broadcasted_iota(jnp.int32, (16, BLK), 0)

    for r in range(ROWB):
        cols = [strips[0][:, r * BLK : (r + 1) * BLK], held[2 * r], held[2 * r + 1]]
        scaled = [
            dot(cols[i], jnp.concatenate(cols[i:], axis=1), 0, 0) * (1.0 / SAMPLES) for i in range(K)
        ]
        for p, (i, j) in enumerate(CROSS):
            at = (j - i) * BLK
            out[r, pl.ds(p * BLK, BLK), :] = scaled[i][:, at : at + BLK].astype(BF16)
        own = [block[:, :BLK] for block in scaled]
        top, bottom = own[2][:HALF], pltpu.roll(own[2][HALF:], HALF, 1)
        folded = jnp.where(row[:HALF] <= col[:HALF], top, bottom)
        out[r, pl.ds(FOLDED, HALF), :] = folded.astype(BF16)
        out[r, pl.ds(MIXED, BLK), :] = jnp.where(row <= col, own[0], own[1]).astype(BF16)
        lines = jnp.zeros((16, BLK), F32)
        for k in range(K):
            diag = jnp.sum(jnp.where(row == col, own[k], 0.0), axis=0, keepdims=True)
            high = diag.astype(BF16).astype(F32)
            lines = jnp.where(line == 2 * k, high, lines)
            lines = jnp.where(line == 2 * k + 1, diag - high, lines)
        out[r, pl.ds(DIAGS, 16), :] = lines.astype(BF16)


def on_strips(kernel, shape, specs, *args):
    arrays = args[len(specs) :]
    samples, columns = arrays[0].shape
    flops = 2 * ROWB * 6 * BLK * BLK * samples
    return pl.pallas_call(
        kernel,
        out_shape=jax.ShapeDtypeStruct(shape, BF16),
        in_specs=specs + [VMEM] * len(arrays),
        out_specs=VMEM,
        scratch_shapes=[pltpu.VMEM((ROWB * (K - 1), samples, BLK), BF16)],
        compiler_params=params(),
        cost_estimate=pl.CostEstimate(flops=flops, bytes_accessed=12 * samples * columns, transcendentals=0),
        name=kernel.__name__,
    )(*args)


def times_gram(packed, high, low):
    total = jnp.zeros((BLK, K * BLK), F32)
    for j in range(K):
        rows = slice(j * BLK, (j + 1) * BLK)
        total += jnp.dot(packed[j], high[rows, :], preferred_element_type=F32)
        total += jnp.dot(packed[j], low[rows, :], preferred_element_type=F32)
    return [total[:, k * BLK : (k + 1) * BLK] for k in range(K)]


def put_squares(grads, out):
    squares = sum(jnp.sum(g * g, axis=0, keepdims=True) for g in grads)
    out[...] = jnp.broadcast_to(squares, out.shape)


def first_kernel(parts, omega, high, low, grad, squares):
    def summed(start, count):
        return sum(parts[s, pl.ds(start, count), :].astype(F32) for s in range(SAMP))

    def put(i, j, block):
        at = (pl.ds(i * BLK, BLK), pl.ds(j * BLK, BLK))
        top = block.astype(BF16)
        high[at] = top
        low[at] = (block - top.astype(F32)).astype(BF16)

    row, col = diagonal_mask()
    lines = summed(DIAGS, 16)
    mixed = summed(MIXED, BLK)
    flipped = mixed.T
    folded = summed(FOLDED, HALF)
    unfolded = jnp.concatenate([folded, pltpu.roll(folded, HALF, 1)], axis=0)
    kept = ((row < HALF) & (row < col)) | ((col >= HALF) & (row > col))
    own = (
        jnp.where(row < col, mixed, flipped),
        jnp.where(row > col, mixed, flipped),
        jnp.where(kept, unfolded, unfolded.T),
    )
    for k in range(K):
        diag = lines[2 * k : 2 * k + 1, :] + lines[2 * k + 1 : 2 * k + 2, :]
        put(k, k, jnp.where(row == col, diag, own[k]))
    for p, (i, j) in enumerate(CROSS):
        block = summed(p * BLK, BLK)
        put(i, j, block)
        put(j, i, block.T)
    grads = times_gram(omega, high, low)
    for k in range(K):
        grad[k] = grads[k]
    put_squares(grads, squares)


def step_of(squares):
    mean_sq = jnp.sum(squares[...]) * (1.0 / ENTRIES)
    mean_sq = jnp.full((8, BLK), mean_sq, F32)
    return (STEP_SCALE / jnp.sqrt(mean_sq + EPSILON))[0:1, :]


def proximal(iterate, grad, step, k):
    stepped = iterate - step * grad
    shrunk = stepped - jnp.clip(stepped, -THRESHOLD, THRESHOLD)
    if k:
        return shrunk
    row, col = diagonal_mask()
    barrier = 0.5 * (stepped + jnp.sqrt(stepped * stepped + 4.0 * step))
    return jnp.where(row == col, barrier, shrunk)


def second_kernel(squares, omega, grad, high, low, iterate, grad2, squares2):
    step = step_of(squares)
    packed = []
    for k in range(K):
        value = proximal(omega[k].astype(F32), grad[k], step, k)
        iterate[k] = value
        packed.append(value.astype(BF16))
    grads = times_gram(packed, high, low)
    for k in range(K):
        grad2[k] = grads[k]
    put_squares(grads, squares2)


def last_kernel(squares, iterate, grad, out):
    step = step_of(squares)
    for k in range(K):
        out[k] = proximal(iterate[k], grad[k], step, k)


def relay_kernel(rows, out):
    out[...] = jnp.broadcast_to(jnp.sum(rows[...], axis=0, keepdims=True), out.shape)


def call(kernel, shapes, *args):
    shapes = [jax.ShapeDtypeStruct(s, d) for s, d in shapes]
    return pl.pallas_call(
        kernel,
        out_shape=shapes,
        in_specs=[VMEM] * len(args),
        out_specs=[VMEM] * len(shapes),
        compiler_params=params(),
        name=kernel.__name__,
    )(*args)


def everywhere(rows):
    rows = lax.all_to_all(rows, ("xh", "y", "xl"), 0, 0, tiled=True)
    (rows,) = call(relay_kernel, [((32, BLK), F32)], rows)
    return lax.all_to_all(rows, ("z", "core"), 0, 0, tiled=True)


def swap(block, axis):
    return lax.ppermute(block, axis, [(0, 1), (1, 0)])


def along_z(block):
    depth, wide = SIZES[0], SIZES[1]
    route = []
    for z in range(depth):
        route.append((z * wide, (z + 1) % depth * wide))
        route.append((z * wide + 1, (z - 1) % depth * wide + 1))
    return lax.ppermute(block, ("z", "xh"), route)


def straight(block):
    depth, wide = SIZES[0], SIZES[1]
    route = []
    for z in range(depth):
        route.append((z * wide + 1, (z + 1) % depth * wide))
        route.append((z * wide, (z - 1) % depth * wide + 1))
    return lax.ppermute(block, ("z", "xh"), route)


def body(observed, pattern, omega_init):
    z, xh, core = (lax.axis_index(a) for a in VAR_AXES)
    samp = lax.axis_index("y") * 2 + lax.axis_index("xl")
    var = (z * 2 + xh) * 2 + core
    var_count = SIZES[0] * 4
    offset = (pattern // ROWB - var + var_count + 2) % var_count - 2
    near = jnp.where((offset == 1) == (core == 0), 1, 3)
    far = jnp.where((offset == 2) == (xh == 0), 2, 4)
    source = jnp.where(offset == 0, 0, jnp.where(abs(offset) == 1, near, far)).astype(jnp.int32)
    column = (pattern % ROWB).astype(jnp.int32)

    edges = [sum(SIZES_OF_CHUNKS[:i]) for i in range(CHUNKS + 1)]
    pieces = [observed[a:b] for a, b in zip(edges, edges[1:])]
    partner = swap(observed, "core")
    across = [swap(a, "xh") for a in pieces]
    beyond = [straight(pieces[0])] + [along_z(a) for a in across[1:]]
    partner, across[0] = lax.optimization_barrier((partner, across[0]))
    here, there = jnp.concatenate(across[:2]), jnp.concatenate(beyond[:2])
    beside = [
        swap(jnp.where(core == xh, here, there), "core"),
        swap(jnp.where(core == xh, across[2], beyond[2]), "core"),
    ]
    strips = [observed, partner, *across, *beside, *beyond]
    grams = on_strips(gram_kernel, (ROWB, GRAM_ROWS, BLK), [SMEM, SMEM], source, column, *strips)
    parts = lax.all_to_all(grams, SAMP_AXES, 0, 0, tiled=True)
    omega = lax.dynamic_index_in_dim(omega_init, samp, 0, keepdims=False)
    side = K * BLK
    blocks = (K, BLK, BLK)
    high, low, grad, squares = call(
        first_kernel,
        [((side, side), BF16), ((side, side), BF16), (blocks, F32), ((16, BLK), F32)],
        parts,
        omega,
    )
    iterate, grad, squares = call(
        second_kernel,
        [(blocks, F32), (blocks, F32), ((16, BLK), F32)],
        everywhere(squares),
        omega,
        grad,
        high,
        low,
    )
    (precision,) = call(last_kernel, [(blocks, F32)], everywhere(squares), iterate, grad)
    return precision[None]


def solution(mesh):
    fine = Mesh(mesh.devices.reshape(SIZES), AXES)
    return jax.shard_map(
        body,
        mesh=fine,
        in_specs=(P(SAMP_AXES, VAR_AXES), P(VAR_AXES, None), P(VAR_AXES, None, None, None)),
        out_specs=P(AXES, None, None, None),
        check_vma=False,
    )
```
